32 devices in a mesh: clip: 2 (over core), span: 4 (over y, x), band: 4 (over z).
Axes of the slice: x: 2, y: 2, z: 4, core: 2. Of those that a mesh axis runs over, the one named last changes fastest.
Arguments:
- frames: bfloat16 [32, 48, 768], P(('clip', 'span'), 'band'), may hold values from -6 to 6
- segments: int32 [8], replicated, may hold values from 0 to 3, never falling along the last dimension, each value on 1 to 4 neighbouring positions
- targets: float32 [4], replicated, may hold values from -4 to 4
- in_weight: bfloat16 [3, 3, 9, 96], replicated, may hold values from -0.625 to 0.625
- in_bias: float32 [96], replicated, may hold values from -2 to 2
- gain_one: float32 [96], replicated, may hold values from 0.1 to 1.9
- mid_weight: bfloat16 [3, 3, 288, 96], replicated, may hold values from -0.125 to 0.125
- mid_bias: float32 [96], replicated, may hold values from -2 to 2
- gain_two: float32 [96], replicated, may hold values from 0.1 to 1.9
- out_weight: bfloat16 [3, 3, 288, 96], replicated, may hold values from -0.125 to 0.125
- out_bias: float32 [96], replicated, may hold values from -2 to 2
- head_weight: float32 [96], replicated, may hold values from -0.625 to 0.625
- head_bias: float32 [1], replicated, may hold values from -3 to 3
Outputs:
- features: bfloat16 [32, 48, 24576], P(('clip', 'span'), 'band')
- scores: float32 [4], replicated
- loss: float32 [], replicated
The draws below stay inside these ranges and needn't reach their ends.
Inputs may be any that keep to these rules, and one draw needn't show every extreme that they name: `segments`: clip numbers never fall along the spans; every clip has 1 to 4 spans and one has exactly 4.
All inputs are finite; a program needn't handle non-finite values.
Results may differ from the reference program's by a relative error of at most 0.008.
Values may be sent and summed in bfloat16 or wider, within the bound.
No kernel may reach another device: no remote copies, remote signals or barrier semaphores. Data moves between devices by JAX's collectives and lax.ppermute only.
A program may use at most 192 MiB of HBM per device.

```python
import math
import jax
import jax.numpy as jnp
import numpy as np
from jax import lax

C = 96
F = 4
W = 256
MAXLEN = 4
SPANS = 8
CLIPS = 4
FRAMES = 32
H = 48


def shard_levels(own_key, extent, shards, least, high):
    def one(axis_at, shards_of):
        draws = jax.random.uniform(jax.random.fold_in(jax.random.fold_in(own_key, 6), axis_at), (shards_of,), jnp.float32, least / len(shards), high / len(shards))
        return jnp.repeat(jnp.exp(draws), extent[axis_at] // shards_of).reshape((-1,) + (1,) * (len(extent) - axis_at - 1))

    loudness = one(*shards[0])
    for cut in shards[1:]:
        loudness = loudness * one(*cut)
    return loudness


def split_up(amount, total, reach, slope):
    weights = [(1 << 20) // math.isqrt(standing ** slope) + 1 for standing in range(2, amount + 1)]
    surplus, given = total - reach - (amount - 1), [1] * (amount - 1)
    while surplus > 0:
        free = [i for i in range(amount - 1) if given[i] < reach]
        mass, remaining = sum([weights[i] for i in free]), surplus
        for i in free:
            more = min(reach - given[i], max(1, remaining * weights[i] // mass), surplus)
            given[i] = given[i] + more
            surplus = surplus - more
    return np.array([reach] + given)


def ragged_sizes(rng, count, total, most, slope):
    if count == 2:
        one = jax.random.randint(rng, (), max(1, total - most), min(most, total - 1) + 1)
        return jnp.stack([one, total - one])
    lengths = jnp.asarray(split_up(count, total, most, slope), jnp.int32)
    pairs = (count - 1) // 2
    giver, receiver = lengths[1:1 + 2 * pairs:2], lengths[2:2 + 2 * pairs:2]
    margin = jnp.minimum(giver - 1, most - receiver)
    shifted = jax.random.randint(jax.random.fold_in(rng, 1), (pairs,), 0, 1 << 20) % (margin + 1)
    lengths = lengths.at[1:1 + 2 * pairs:2].set(giver - shifted).at[2:2 + 2 * pairs:2].set(receiver + shifted)
    return lengths[jax.random.permutation(jax.random.fold_in(rng, 2), count)]


def bell_draw(key, extent, deviation, most, split=(), kind=jnp.bfloat16):
    array = jax.random.normal(key, extent, jnp.float32) * deviation
    if len(split) > 0:
        array = shard_levels(key, extent, split, -0.22, 0.18) * array
    return jnp.clip(array, min=-most, max=most).astype(kind)


def setup_inputs(seed: int = 0) -> dict:
    arg_keys = jax.random.split(jax.random.key(seed), 14)
    frames = bell_draw(arg_keys[0], (FRAMES, H, W * 3), 1.0, 6.0, ((0, 8), (1, 4)))
    segments = jnp.searchsorted(jnp.cumsum(ragged_sizes(arg_keys[1], CLIPS, SPANS, MAXLEN, 1)), jnp.arange(SPANS), side="right").astype(jnp.int32)
    targets = bell_draw(arg_keys[2], (CLIPS,), 1.0, 4.0, (), jnp.float32)
    in_weight = bell_draw(arg_keys[3], (3, 3, 9, C), 81 ** -0.5, 0.625)
    in_bias = bell_draw(arg_keys[4], (C,), 0.3, 2.0, (), jnp.float32)
    gain_one = jnp.clip(1.0 + 0.18 * jax.random.normal(arg_keys[5], (C,), jnp.float32), 0.1, 1.9)
    mid_weight = bell_draw(arg_keys[6], (3, 3, 3 * C, C), (27 * C) ** -0.5, 0.125)
    mid_bias = bell_draw(arg_keys[7], (C,), 0.3, 2.0, (), jnp.float32)
    gain_two = jnp.clip(1.0 + 0.18 * jax.random.normal(arg_keys[8], (C,), jnp.float32), 0.1, 1.9)
    out_weight = bell_draw(arg_keys[9], (3, 3, 3 * C, C), (27 * C) ** -0.5, 0.125)
    out_bias = bell_draw(arg_keys[10], (C,), 0.3, 2.0, (), jnp.float32)
    head_weight = bell_draw(arg_keys[11], (C,), C ** -0.5, 0.625, (), jnp.float32)
    head_bias = bell_draw(arg_keys[12], (1,), 1.0, 3.0, (), jnp.float32)
    return dict(frames=frames, segments=segments, targets=targets, in_weight=in_weight, in_bias=in_bias, gain_one=gain_one, mid_weight=mid_weight, mid_bias=mid_bias, gain_two=gain_two, out_weight=out_weight, out_bias=out_bias, head_weight=head_weight, head_bias=head_bias)


def apply_taps(wide, weight, count, rows):
    total = None
    for dt in range(3):
        for dr in range(3):
            part = jnp.einsum('frwc,cd->frwd', wide[dt:dt + count, dr:dr + rows].astype(jnp.float32), weight[dt, dr].astype(jnp.float32))
            total = part if total is None else total + part
    return total

def causal_conv(source, weight, keep):
    padded = jnp.pad(source, ((2, 0), (1, 1), (1, 1), (0, 0)))

    def one_span(index):
        ext = lax.dynamic_slice_in_dim(padded, (index * F).astype(jnp.int32), F + 2, 0)
        scale = jnp.concatenate([jnp.full((2,), keep[index], jnp.float32), jnp.ones((F,), jnp.float32)]).astype(source.dtype)
        ext = ext * scale[:, None, None, None]
        wide = jnp.concatenate([ext[:, :, k:k + W] for k in range(3)], axis=3)
        return apply_taps(wide, weight, F, H)
    out = lax.map(one_span, jnp.arange(SPANS, dtype=jnp.int32))
    return out.reshape(FRAMES, H, W, -1)

def rms_silu(value, gain):
    normed = value * lax.rsqrt(lax.optimization_barrier(jnp.mean(value * value, axis=-1, keepdims=True)) + 1e-06) * gain
    return jax.nn.silu(normed)

def reference(frames, segments, targets, in_weight, in_bias, gain_one, mid_weight, mid_bias, gain_two, out_weight, out_bias, head_weight, head_bias):
    previous = jnp.concatenate([segments[:1] - 1, segments[:-1]])
    keep = (segments == previous).astype(jnp.float32)
    pixels = frames.reshape(FRAMES, H, W, 3)
    h0 = (causal_conv(pixels, in_weight, keep) + in_bias).astype(jnp.bfloat16)
    act_one = rms_silu(h0.astype(jnp.float32), gain_one).astype(jnp.bfloat16)
    h1 = causal_conv(act_one, mid_weight, keep) + mid_bias
    act_two = rms_silu(h1, gain_two).astype(jnp.bfloat16)
    features = (h0.astype(jnp.float32) + causal_conv(act_two, out_weight, keep) + out_bias).astype(jnp.bfloat16)
    span_sums = lax.optimization_barrier(jnp.sum(features.astype(jnp.float32).reshape(SPANS, F * H * W, C), axis=1))
    member = (segments[:, None] == jnp.arange(CLIPS, dtype=jnp.int32)[None, :]).astype(jnp.float32)
    totals = jnp.dot(member.T, span_sums, precision=lax.Precision.HIGHEST)
    cells = lax.optimization_barrier(jnp.sum(member, axis=0)) * (F * H * W)
    pooled = totals / cells[:, None]
    scores = jnp.dot(pooled, head_weight, precision=lax.Precision.HIGHEST) + head_bias[0]
    loss = jnp.mean((scores - targets) ** 2)
    return (features.reshape(FRAMES, H, W * C), scores, loss)
```

```python
import functools

import jax
import jax.numpy as jnp
from jax import lax
from jax.experimental import pallas as pl
from jax.experimental.pallas import tpu as pltpu
from jax.sharding import PartitionSpec as P

BF16 = jnp.bfloat16
F32 = jnp.float32
POSITION = ("clip", "span")
SLOT = 32


def moved(block, axis, distance):
    count = lax.axis_size(axis)
    route = [(i, i + distance) for i in range(count) if 0 <= i + distance < count]
    return lax.ppermute(block, axis, route)


def total_over(value, axis):
    count = lax.axis_size(axis)
    if count & (count - 1):
        return lax.psum(value, axis)
    step = 1
    while step < count:
        value = value + lax.ppermute(value, axis, [(i, i ^ step) for i in range(count)])
        step *= 2
    return value


def shifted_sum(product, channels, first, last):
    width = product.shape[1]
    left = jnp.where(first, 0.0, pltpu.roll(product[:channels], 1, 1))
    right = jnp.where(last, 0.0, pltpu.roll(product[2 * channels :], width - 1, 1))
    return product[channels : 2 * channels] + left + right


def rms_silu(value, gain):
    scale = lax.rsqrt(jnp.mean(value * value, axis=0, keepdims=True) + 1e-06)
    half = value * scale * (0.5 * gain)
    return half + half * jnp.tanh(half)


def block_kernel(
    flags, x_ref, win_ref, wmid_ref, wout_ref, cols_ref, out_ref, sum_ref,
    act_one, act_two, h0_ref, table, total, stage,
):
    rows, count = out_ref.shape[0], out_ref.shape[1]
    channels = win_ref.shape[0]
    width = x_ref.shape[3]
    keep, top, bottom = flags[0], flags[1], flags[2]

    columns = jnp.transpose(cols_ref[...])
    for j in range(6):
        table[j] = jnp.broadcast_to(columns[:, j : j + 1], (channels, width))
    total[...] = jnp.zeros_like(total)
    pixel = lax.broadcasted_iota(jnp.int32, (channels, width), 1)
    first, last = pixel == 0, pixel == width - 1

    def row_mask(row, rim, extent):
        inside = jnp.where(row < rim, top, 1.0)
        return inside * jnp.where(row >= extent - rim, bottom, 1.0)

    def first_row(row, carry):
        mask = row_mask(row, 2, rows + 4)
        for t in range(count + 4):
            taps = x_ref[t : t + 3, row].reshape(3 * SLOT, width)
            h0 = jnp.dot(win_ref[...], taps, preferred_element_type=F32) + table[0]
            h0 = h0.astype(BF16)
            if t >= 4:
                h0_ref[row, t - 4] = h0
            act = rms_silu(h0.astype(F32), table[1]) * (mask * keep if t < 4 else mask)
            act_one[row, t] = act.astype(BF16)
        return carry

    lax.fori_loop(0, rows + 4, first_row, 0)

    def taps_of(source, row, t):
        return jnp.concatenate(
            [source[row + dr, t : t + 3].reshape(3 * channels, width) for dr in range(3)], axis=0
        )

    def middle_row(row, carry):
        mask = row_mask(row, 1, rows + 2)
        for t in range(count + 2):
            product = jnp.dot(wmid_ref[...], taps_of(act_one, row, t), preferred_element_type=F32)
            h1 = shifted_sum(product, channels, first, last) + table[2]
            act = rms_silu(h1, table[3]) * (mask * keep if t < 2 else mask)
            act_two[row, t] = act.astype(BF16)
        return carry

    lax.fori_loop(0, rows + 2, middle_row, 0)

    lane = lax.broadcasted_iota(jnp.int32, (width // 4, count, 128), 2)

    def last_row(row, carry):
        for t in range(count):
            product = jnp.dot(wout_ref[...], taps_of(act_two, row, t), preferred_element_type=F32)
            value = shifted_sum(product, channels, first, last) + table[4]
            value = (value + h0_ref[row + 2, t].astype(F32)).astype(BF16).astype(F32)
            total[...] += value
            padded = jnp.concatenate([value, jnp.zeros((128 - channels, width), F32)], axis=0)
            stage[:, t, :] = jnp.transpose(padded)
        pixels = stage[...].reshape(width // 4, 4, count, 128)
        one = pltpu.roll(pixels[:, 1], 96, 2)
        two = pltpu.roll(pixels[:, 2], 64, 2)
        three = pltpu.roll(pixels[:, 3], 32, 2)
        tiles = [
            jnp.where(lane < 96, pixels[:, 0], one).astype(BF16),
            jnp.where(lane < 64, one, two).astype(BF16),
            jnp.where(lane < 32, two, three).astype(BF16),
        ]
        for group in range(width // 4):
            for j in range(3):
                at = (3 * group + j) * 128
                out_ref[row, :, at : at + 128] = tiles[j][group]
        return carry

    lax.fori_loop(0, rows, last_row, 0)
    sum_ref[...] = jnp.broadcast_to(jnp.sum(total[...] * table[5], keepdims=True), sum_ref.shape)


def local(
    frames, segments, targets, in_weight, in_bias, gain_one, mid_weight, mid_bias,
    gain_two, out_weight, out_bias, head_weight, head_bias,
):
    count, rows = frames.shape[0], frames.shape[1]
    channels = in_bias.shape[0]
    width = frames.shape[2] // 3
    position = lax.axis_index(POSITION)
    band = lax.axis_index("band")
    clip_id = segments[position]
    before = segments[jnp.maximum(position - 1, 0)]
    keep = ((position > 0) & (clip_id == before)).astype(F32)
    older = segments[jnp.maximum(position - 2, 0)]
    keep_older = ((position > 1) & (older == before)).astype(F32) * keep
    flags = jnp.stack(
        [keep, (band > 0).astype(F32), (band < lax.axis_size("band") - 1).astype(F32)]
    )

    colours = frames.reshape(count, rows, width, 3).transpose(0, 1, 3, 2)
    low = moved(colours[:, rows - 3 :], "band", 1)
    high = moved(colours[:, :3], "band", -1)
    wide = jnp.concatenate([low, colours, high], axis=1)
    previous = moved(wide, POSITION, 1) * keep.astype(BF16)
    oldest = moved(wide[count - 2 :], POSITION, 2) * keep_older.astype(BF16)
    wide = jnp.concatenate([oldest, previous, wide], axis=0)
    spread = jnp.pad(wide, ((0, 0), (0, 0), (0, 0), (1, 1)))
    spread = jnp.concatenate([spread[..., k : k + width] for k in range(3)], axis=2)
    taps = [spread[:, dr : dr + rows + 4] for dr in range(3)]
    taps.append(jnp.zeros(taps[0].shape[:2] + (SLOT - 27, width), BF16))
    taps = jnp.concatenate(taps, axis=2)

    win = jnp.pad(in_weight.reshape(3, 27, channels), ((0, 0), (0, SLOT - 27), (0, 0)))
    win = win.reshape(3 * SLOT, channels).T

    def side_by_side(weight):
        weight = weight.reshape(3, 3, 3, channels, channels)
        return weight.transpose(2, 4, 1, 0, 3).reshape(3 * channels, 9 * channels)

    cols = jnp.stack(
        [in_bias, gain_one, mid_bias, gain_two, out_bias, head_weight, in_bias, in_bias]
    )
    vmem = pl.BlockSpec(memory_space=pltpu.VMEM)
    features, weighted = pl.pallas_call(
        block_kernel,
        in_specs=[pl.BlockSpec(memory_space=pltpu.SMEM)] + [vmem] * 5,
        out_specs=[vmem, vmem],
        out_shape=[
            jax.ShapeDtypeStruct((rows, count, width * channels), BF16),
            jax.ShapeDtypeStruct((1, 128), F32),
        ],
        scratch_shapes=[
            pltpu.VMEM((rows + 4, count + 4, channels, width), BF16),
            pltpu.VMEM((rows + 2, count + 2, channels, width), BF16),
            pltpu.VMEM((rows + 4, count, channels, width), BF16),
            pltpu.VMEM((6, channels, width), F32),
            pltpu.VMEM((channels, width), F32),
            pltpu.VMEM((width, count, 128), F32),
        ],
        compiler_params=pltpu.CompilerParams(vmem_limit_bytes=56 << 20),
    )(flags, taps, win, side_by_side(mid_weight), side_by_side(out_weight), cols)
    features = features.transpose(1, 0, 2)

    labels = jnp.arange(targets.shape[0], dtype=jnp.int32)
    part = jnp.where(labels == clip_id, weighted[0, 0], 0.0)
    for axis in ("band", "span", "clip"):
        part = total_over(part, axis)
    member = (segments[:, None] == labels[None, :]).astype(F32)
    cells = jnp.sum(member, axis=0) * (count * rows * lax.axis_size("band") * width)
    scores = part / cells + head_bias[0]
    loss = jnp.mean((scores - targets) ** 2)
    return features, scores, loss


def solution(mesh):
    split = P(POSITION, "band", None)
    return jax.shard_map(
        local,
        mesh=mesh,
        in_specs=(split,) + (P(),) * 12,
        out_specs=(split, P(), P()),
        check_vma=False,
    )
```

```python
import jax
import jax.numpy as jnp
from jax import lax
from jax.experimental import pallas as pl
from jax.experimental.pallas import tpu as pltpu
from jax.sharding import PartitionSpec as P

BF16 = jnp.bfloat16
F32 = jnp.float32
POSITION = ("clip", "span")
EVERY = ("clip", "span", "band")
SLOT = 16
SPAN_SLOTS = 16


def moved(block, axis, distance):
    count = lax.axis_size(axis)
    route = [(i, i + distance) for i in range(count) if 0 <= i + distance < count]
    return lax.ppermute(block, axis, route)


def shifted_sum(product, channels, first, last):
    width = product.shape[1]
    left = jnp.where(first, 0.0, pltpu.roll(product[:channels], 1, 1))
    right = jnp.where(last, 0.0, pltpu.roll(product[2 * channels :], width - 1, 1))
    return product[channels : 2 * channels] + left + right


def rms_silu(value, gain):
    scale = lax.rsqrt(jnp.mean(value * value, axis=0, keepdims=True) + 1e-06)
    half = value * scale * (0.5 * gain)
    return half + half * jnp.tanh(half)


def block_kernel(
    seg_ref, x_ref, win_ref, wmid_ref, wout_ref, cols_ref, out_ref, sum_ref,
    planes, inputs, win, wmid, wout, act_one, act_two, h0_ref, table, total, stage,
):
    rows, count = out_ref.shape[0], out_ref.shape[1]
    channels = cols_ref.shape[1]
    width = inputs.shape[3]
    pairs = width // 2
    position, band = lax.axis_index(POSITION), lax.axis_index("band")
    clip_id = seg_ref[position]
    before = seg_ref[jnp.maximum(position - 1, 0)]
    older = seg_ref[jnp.maximum(position - 2, 0)]
    keep = jnp.where((position > 0) & (clip_id == before), 1.0, 0.0)
    keep_older = jnp.where((position > 1) & (older == before), keep, 0.0)
    top = jnp.where(band > 0, 1.0, 0.0)
    bottom = jnp.where(band < lax.axis_size("band") - 1, 1.0, 0.0)

    unit = jnp.where(
        lax.broadcasted_iota(jnp.int32, (channels, channels), 0)
        == lax.broadcasted_iota(jnp.int32, (channels, channels), 1), 1.0, 0.0,
    ).astype(BF16)

    def turned(weight):
        return lax.dot_general(
            unit, weight, (((1,), (1,)), ((), ())), preferred_element_type=F32
        ).astype(BF16)

    for source, target in ((wmid_ref, wmid), (wout_ref, wout)):
        for k in range(3):
            piece = [
                source[dt, dr, k * channels : (k + 1) * channels]
                for dr in range(3) for dt in range(3)
            ]
            target[k * channels : (k + 1) * channels] = turned(jnp.concatenate(piece, axis=0))
    win[...] = turned(win_ref[...])
    columns = jnp.transpose(cols_ref[...])
    for j in range(6):
        table[j] = jnp.broadcast_to(columns[:, j : j + 1], (channels, width))
    total[...] = jnp.zeros_like(total)

    span = 3 * pairs
    lane = lax.broadcasted_iota(jnp.int32, (span, span), 1)
    pick = lax.broadcasted_iota(jnp.int32, (span, span), 0) == 3 * (lane % pairs) + lane // pairs
    pick = jnp.where(pick, 1.0, 0.0).astype(BF16)
    frames = x_ref.shape[0] * x_ref.shape[1]
    flat = x_ref[...].reshape(frames, x_ref.shape[2])
    halves = [
        jnp.dot(flat[:, h * span : (h + 1) * span], pick, preferred_element_type=F32)
        for h in range(2)
    ]
    slot = lax.broadcasted_iota(jnp.int32, (frames, width), 0) % SPAN_SLOTS
    kept = jnp.where(slot < 2, keep_older, jnp.where(slot < 6, keep, 1.0))
    pixel = lax.broadcasted_iota(jnp.int32, (frames, width), 1)
    for c in range(3):
        plane = jnp.concatenate([h[:, c * pairs : (c + 1) * pairs] for h in halves], axis=1) * kept
        planes[:, c, :] = jnp.where(pixel == 0, 0.0, pltpu.roll(plane, 1, 1))
        planes[:, 3 + c, :] = plane
        planes[:, 6 + c, :] = jnp.where(pixel == width - 1, 0.0, pltpu.roll(plane, width - 1, 1))
    for c in range(9, SLOT):
        planes[:, c, :] = jnp.zeros((frames, width), F32)

    def narrow(row, carry):
        at = pl.multiple_of(row * SPAN_SLOTS, SPAN_SLOTS)
        inputs[row] = planes[pl.ds(at, SPAN_SLOTS)].astype(BF16)
        return carry

    lax.fori_loop(0, rows + 6, narrow, 0)

    pixel = lax.broadcasted_iota(jnp.int32, (channels, width), 1)
    first, last = pixel == 0, pixel == width - 1

    def row_mask(row, rim, extent):
        inside = jnp.where(row < rim, top, 1.0)
        return inside * jnp.where(row >= extent - rim, bottom, 1.0)

    def taps_of(source, row, t):
        depth = 3 * source.shape[2]
        return jnp.concatenate(
            [source[row + dr, t : t + 3].reshape(depth, width) for dr in range(3)], axis=0
        )

    def first_row(row):
        mask = row_mask(row, 2, rows + 4)
        for t in range(count + 4):
            h0 = jnp.dot(win[...], taps_of(inputs, row, t), preferred_element_type=F32)
            h0 = (h0 + table[0]).astype(BF16)
            if t >= 4:
                h0_ref[row, t - 4] = h0
            act = rms_silu(h0.astype(F32), table[1]) * (mask * keep if t < 4 else mask)
            act_one[row, t] = act.astype(BF16)

    def middle_row(row):
        mask = row_mask(row, 1, rows + 2)
        for t in range(count + 2):
            product = jnp.dot(wmid[...], taps_of(act_one, row, t), preferred_element_type=F32)
            h1 = shifted_sum(product, channels, first, last) + table[2]
            act = rms_silu(h1, table[3]) * (mask * keep if t < 2 else mask)
            act_two[row, t] = act.astype(BF16)

    def last_row(row):
        for t in range(count):
            product = jnp.dot(wout[...], taps_of(act_two, row, t), preferred_element_type=F32)
            value = shifted_sum(product, channels, first, last) + table[4]
            value = (value + h0_ref[row + 2, t].astype(F32)).astype(BF16).astype(F32)
            total[...] += value
            padded = jnp.concatenate([value, jnp.zeros((128 - channels, width), F32)], axis=0)
            stage[:, t, :] = jnp.transpose(padded)

    lanes = lax.broadcasted_iota(jnp.int32, (width // 4, count, 128), 2)

    def written(row):
        pixels = stage[...].reshape(width // 4, 4, count, 128)
        one = pltpu.roll(pixels[:, 1], 96, 2)
        two = pltpu.roll(pixels[:, 2], 64, 2)
        three = pltpu.roll(pixels[:, 3], 32, 2)
        tiles = [
            jnp.where(lanes < 96, pixels[:, 0], one).astype(BF16),
            jnp.where(lanes < 64, one, two).astype(BF16),
            jnp.where(lanes < 32, two, three).astype(BF16),
        ]
        for group in range(width // 4):
            for j in range(3):
                at = (3 * group + j) * 128
                out_ref[row, :, at : at + 128] = tiles[j][group]

    def loop(begin, end, *steps):
        def body(row, carry):
            for step, lag in steps:
                step(row + lag)
            return carry

        lax.fori_loop(begin, end, body, 0)

    loop(0, 3, (first_row, 0))
    loop(0, 3, (first_row, 3), (middle_row, 0))
    written_before = lambda row: written(jnp.maximum(row - 1, 0))
    loop(0, rows - 2, (written_before, 0), (first_row, 6), (last_row, 0), (middle_row, 3))
    loop(rows - 2, rows - 1, (written_before, 0), (last_row, 0), (middle_row, 3))
    loop(rows - 1, rows, (written_before, 0), (last_row, 0))
    written(rows - 1)
    clip = lax.broadcasted_iota(jnp.int32, sum_ref.shape, 1)
    weighted = jnp.sum(total[...] * table[5], keepdims=True)
    sum_ref[...] = jnp.where(clip == clip_id, jnp.broadcast_to(weighted, sum_ref.shape), 0.0)


def local(
    frames, segments, targets, in_weight, in_bias, gain_one, mid_weight, mid_bias,
    gain_two, out_weight, out_bias, head_weight, head_bias,
):
    count, rows = frames.shape[0], frames.shape[1]
    channels = in_bias.shape[0]
    width = frames.shape[2] // 3
    devices = lax.axis_size(EVERY)

    own = frames.transpose(1, 0, 2)
    low = moved(own[rows - 3 :], "band", 1)
    high = moved(own[:3], "band", -1)
    wide = jnp.concatenate([low, own, high], axis=0)
    previous = moved(wide, POSITION, 1)
    oldest = moved(wide[:, count - 2 :], POSITION, 2)
    unused = jnp.zeros((rows + 6, SPAN_SLOTS - 2 * count - 2, 3 * width), BF16)
    seen = jnp.concatenate([oldest, previous, wide, unused], axis=1)

    win = jnp.pad(in_weight, ((0, 0), (0, 0), (0, SLOT - 9), (0, 0)))
    win = win.transpose(1, 0, 2, 3).reshape(9 * SLOT, channels)
    cols = jnp.stack(
        [in_bias, gain_one, mid_bias, gain_two, out_bias, head_weight, in_bias, in_bias]
    )
    vmem = pl.BlockSpec(memory_space=pltpu.VMEM)
    features, weighted = pl.pallas_call(
        block_kernel,
        in_specs=[pl.BlockSpec(memory_space=pltpu.SMEM)] + [vmem] * 5,
        out_specs=[vmem, vmem],
        out_shape=[
            jax.ShapeDtypeStruct((rows, count, width * channels), BF16),
            jax.ShapeDtypeStruct((devices, 128), F32),
        ],
        scratch_shapes=[
            pltpu.VMEM(((rows + 6) * SPAN_SLOTS, SLOT, width), F32),
            pltpu.VMEM((rows + 6, SPAN_SLOTS, SLOT, width), BF16),
            pltpu.VMEM((channels, 9 * SLOT), BF16),
            pltpu.VMEM((3 * channels, 9 * channels), BF16),
            pltpu.VMEM((3 * channels, 9 * channels), BF16),
            pltpu.VMEM((rows + 4, count + 4, channels, width), BF16),
            pltpu.VMEM((rows + 2, count + 2, channels, width), BF16),
            pltpu.VMEM((rows + 4, count, channels, width), BF16),
            pltpu.VMEM((6, channels, width), F32),
            pltpu.VMEM((channels, width), F32),
            pltpu.VMEM((width, count, 128), F32),
        ],
        compiler_params=pltpu.CompilerParams(vmem_limit_bytes=56 << 20),
    )(segments, seen, win, mid_weight, out_weight, cols)
    features = features.transpose(1, 0, 2)

    clips = targets.shape[0]
    gathered = lax.all_to_all(weighted, EVERY, 0, 0, tiled=True)
    part = jnp.sum(gathered[:, :clips], axis=0)
    labels = jnp.arange(clips, dtype=jnp.int32)
    member = (segments[:, None] == labels[None, :]).astype(F32)
    cells = jnp.sum(member, axis=0) * (count * rows * lax.axis_size("band") * width)
    scores = part / cells + head_bias[0]
    loss = jnp.mean((scores - targets) ** 2)
    return features, scores, loss


def solution(mesh):
    split = P(POSITION, "band", None)
    return jax.shard_map(
        local,
        mesh=mesh,
        in_specs=(split,) + (P(),) * 12,
        out_specs=(split, P(), P()),
        check_vma=False,
    )
```

```python
import functools

import jax
import jax.numpy as jnp
from jax import lax
from jax.experimental import pallas as pl
from jax.experimental.pallas import tpu as pltpu
from jax.sharding import PartitionSpec as P

BF16 = jnp.bfloat16
F32 = jnp.float32
POSITION = ("clip", "span")
EVERY = ("clip", "span", "band")
SLOTS = 8


def moved(block, axis, distance):
    count = lax.axis_size(axis)
    route = [(i, i + distance) for i in range(count) if 0 <= i + distance < count]
    return lax.ppermute(block, axis, route)


def shifted_sum(product, channels):
    left, middle, right = (product[k * channels : (k + 1) * channels] for k in range(3))
    lane = lax.broadcasted_iota(jnp.int32, (channels, 128), 1)
    tiles = product.shape[1] // 128
    cut = [slice(i * 128, (i + 1) * 128) for i in range(tiles)]
    left = [pltpu.roll(left[:, c], 1, 1) for c in cut]
    right = [pltpu.roll(right[:, c], 127, 1) for c in cut]
    parts = []
    for i in range(tiles):
        low = jnp.where(lane == 0, left[i - 1] if i else 0.0, left[i])
        high = jnp.where(lane == 127, right[i + 1] if i + 1 < tiles else 0.0, right[i])
        parts.append(middle[:, cut[i]] + low + high)
    return jnp.concatenate(parts, axis=1)


def rms_silu(value, half_gain, mask):
    scale = lax.rsqrt(jnp.mean(value * value, axis=0, keepdims=True) + 1e-06) * mask
    half = value * scale * half_gain
    return half + half * jnp.tanh(half)


def pipelined(units):
    waiting = []
    for start, ends in units:
        product = start()
        for end in waiting:
            end()
        waiting = [functools.partial(end, product) for end in ends]
    for end in waiting:
        end()


def block_kernel(
    seg_ref, own_ref, previous_ref, oldest_ref, low_ref, high_ref,
    win_ref, wmid_ref, wout_ref, cols_ref, out_ref, sum_ref,
    gathered, planes, win, wmid, wout, act_one, act_two, h0_ref, table, total, stage, order,
    tiles_ref,
):
    rows, count = out_ref.shape[0], out_ref.shape[1]
    channels = cols_ref.shape[1]
    width = own_ref.shape[2] // 3
    pairs = width // 2
    position, band = lax.axis_index(POSITION), lax.axis_index("band")
    clip_id = seg_ref[position]
    before = seg_ref[jnp.maximum(position - 1, 0)]
    older = seg_ref[jnp.maximum(position - 2, 0)]
    keep = jnp.where((position > 0) & (clip_id == before), 1.0, 0.0)
    keep_older = jnp.where((position > 1) & (older == before), keep, 0.0)
    top = jnp.where(band > 0, 1.0, 0.0)
    bottom = jnp.where(band < lax.axis_size("band") - 1, 1.0, 0.0)

    unit = jnp.where(
        lax.broadcasted_iota(jnp.int32, (channels, channels), 0)
        == lax.broadcasted_iota(jnp.int32, (channels, channels), 1), 1.0, 0.0,
    ).astype(BF16)

    def turned(weight):
        return lax.dot_general(
            unit, weight, (((1,), (1,)), ((), ())), preferred_element_type=F32
        ).astype(BF16)

    for source, target in ((wmid_ref, wmid), (wout_ref, wout)):
        for k in range(3):
            piece = [
                source[dt, dr, k * channels : (k + 1) * channels]
                for dr in range(3) for dt in range(3)
            ]
            target[k * channels : (k + 1) * channels] = turned(jnp.concatenate(piece, axis=0))
    bias = cols_ref[:1]
    high = bias.astype(BF16).astype(F32)
    middle = (bias - high).astype(BF16).astype(F32)
    low = bias - high - middle
    bias = jnp.concatenate([high, middle, low, jnp.zeros((5, channels), F32)], axis=0)
    for t in range(count):
        piece = pltpu.roll(win_ref[...], t, 1) if t else win_ref[...]
        piece = jnp.concatenate([piece.reshape(27 * SLOTS, channels), bias], axis=0)
        win[t * channels : (t + 1) * channels] = turned(piece.astype(BF16))
    columns = jnp.transpose(cols_ref[...])
    for j in range(6):
        column = columns[:, j : j + 1] * (0.5 if j in (1, 3) else 1.0)
        table[j] = jnp.broadcast_to(column, (channels, width))
    total[...] = jnp.zeros_like(total)

    span = 3 * pairs
    lane = lax.broadcasted_iota(jnp.int32, (span, span), 1)
    pick = lax.broadcasted_iota(jnp.int32, (span, span), 0) == 3 * (lane % pairs) + lane // pairs
    pick = jnp.where(pick, 1.0, 0.0).astype(BF16)
    sources = ((0, oldest_ref, 6, 2, 4), (2, previous_ref, 3, 0, 4), (6, own_ref, 0, 0, 2),
               (8, previous_ref, 3, 2, 4), (10, own_ref, 0, 0, 4))
    for at, source, rim, begin, end in sources:
        to = slice(at, at + end - begin)
        gathered[3 : rows + 3, to] = source[:, begin:end].astype(F32)
        gathered[:3, to] = low_ref[rim : rim + 3, begin:end].astype(F32)
        gathered[rows + 3 :, to] = high_ref[rim : rim + 3, begin:end].astype(F32)
    gathered[:, 14:] = jnp.zeros((rows + 6, 2, 3 * width), F32)
    frames = (rows + 6) * 2 * SLOTS
    flat = gathered[...].reshape(frames, 3 * width).astype(BF16)
    halves = [
        jnp.dot(flat[:, h * span : (h + 1) * span], pick, preferred_element_type=F32)
        for h in range(2)
    ]
    slot = lax.broadcasted_iota(jnp.int32, (frames, width), 0) % (2 * SLOTS)
    kept = jnp.where((slot < 6) | (slot == 8) | (slot == 9), keep, 1.0)
    kept = jnp.where(slot < 2, keep_older, kept)
    pixel = lax.broadcasted_iota(jnp.int32, (frames, width), 1)
    for c in range(3):
        plane = jnp.concatenate([h[:, c * pairs : (c + 1) * pairs] for h in halves], axis=1) * kept
        planes[c] = jnp.where(pixel == 0, 0.0, pltpu.roll(plane, 1, 1)).reshape(planes.shape[1:])
        planes[3 + c] = plane.reshape(planes.shape[1:])
        plane = jnp.where(pixel == width - 1, 0.0, pltpu.roll(plane, width - 1, 1))
        planes[6 + c] = plane.reshape(planes.shape[1:])

    part = width // 4
    row = lax.broadcasted_iota(jnp.int32, (width, width), 0)
    pixel = row % part // count * 4 + row // part
    wanted = row % count * part + pixel
    hit = lax.broadcasted_iota(jnp.int32, (width, width), 1) == wanted
    order[...] = jnp.where(hit, 1.0, 0.0).astype(BF16)
    stage[...] = jnp.zeros_like(stage)

    def row_mask(row, rim, extent):
        inside = jnp.where(row < rim, top, 1.0)
        return inside * jnp.where(row >= extent - rim, bottom, 1.0)

    def taps_of(source, row, t):
        return jnp.concatenate(
            [source[row + dr, t : t + 3].reshape(3 * channels, width) for dr in range(3)], axis=0
        )

    def first_units(row):
        mask = row_mask(row, 2, rows + 4)

        def end(t, at, product):
            h0 = product[at : at + channels].astype(BF16)
            if t >= 4:
                h0_ref[row, t - 4] = h0
            act = rms_silu(h0.astype(F32), table[1], mask * keep if t < 4 else mask)
            act_one[row, t] = act.astype(BF16)

        def start(half):
            taps = planes[:, pl.ds(row, 3), half * SLOTS : (half + 1) * SLOTS]
            taps = [taps.reshape(27 * SLOTS, width), jnp.ones((SLOTS, width), F32)]
            taps = jnp.concatenate(taps, axis=0).astype(BF16)
            return jnp.dot(win[...], taps, preferred_element_type=F32)

        return [
            (
                functools.partial(start, half),
                [functools.partial(end, count * half + t, t * channels) for t in range(count)],
            )
            for half in range(2)
        ]

    def middle_units(row):
        mask = row_mask(row, 1, rows + 2)

        def start(t):
            return jnp.dot(wmid[...], taps_of(act_one, row, t), preferred_element_type=F32)

        def end(t, product):
            h1 = shifted_sum(product, channels) + table[2]
            act = rms_silu(h1, table[3], mask * keep if t < 2 else mask)
            act_two[row, t] = act.astype(BF16)

        return [
            (functools.partial(start, t), [functools.partial(end, t)]) for t in range(count + 2)
        ]

    def last_units(row):
        def start(t):
            return jnp.dot(wout[...], taps_of(act_two, row, t), preferred_element_type=F32)

        def end(t, product):
            value = shifted_sum(product, channels) + table[4]
            value = (value + h0_ref[row + 2, t].astype(F32)).astype(BF16)
            total[...] += value.astype(F32)
            stage[t, :channels] = value

        return [(functools.partial(start, t), [functools.partial(end, t)]) for t in range(count)]

    def written_units():
        lane = lax.broadcasted_iota(jnp.int32, (128, 128), 1)

        def start(piece):
            half = slice(piece // 2 * 128, piece // 2 * 128 + 128)
            sides = []
            for t in range(0, count, 2):
                one, two = stage[t, :, half].astype(F32), stage[t + 1, :, half].astype(F32)
                if piece % 2:
                    one = pltpu.roll(one, part, 1)
                else:
                    two = pltpu.roll(two, part, 1)
                sides.append(jnp.where(lane < part, one, two).astype(BF16))
            return lax.dot_general(
                order[...], jnp.concatenate(sides, axis=1), (((1,), (1,)), ((), ())),
                preferred_element_type=F32,
            )

        def end(piece, product):
            pixels = [product[i * part : (i + 1) * part] for i in range(4)]
            pixels = [pltpu.roll(x, 128 - 32 * i, 1) if i else x for i, x in enumerate(pixels)]
            lane = lax.broadcasted_iota(jnp.int32, (part, 128), 1)
            for j in range(3):
                tile = jnp.where(lane < 96 - 32 * j, pixels[j], pixels[j + 1])
                for group in range(part // count):
                    at = (3 * (piece * part // count + group) + j) * 128
                    tiles_ref[:, at : at + 128] = tile[group * count : (group + 1) * count]

        return [
            (functools.partial(start, piece), [functools.partial(end, piece)])
            for piece in range(4)
        ]

    def written(row):
        out_ref[row] = tiles_ref[...].astype(BF16)

    def mixed(first, second):
        units = []
        for i in range(max(len(first), len(second))):
            units += first[i : i + 1] + second[i : i + 1]
        return units

    def loop(begin, end, body):
        def step(row, carry):
            body(row)
            return carry

        lax.fori_loop(begin, end, step, 0)

    loop(0, 3, lambda row: pipelined(first_units(row)))
    loop(0, 3, lambda row: pipelined(mixed(middle_units(row), first_units(row + 3))))

    def steady(row, middle=True, first=True):
        units = mixed(written_units(), middle_units(row + 3) if middle else [])
        units += mixed(last_units(row), first_units(row + 6) if first else [])
        pipelined(units)
        written(jnp.maximum(row - 1, 0))

    loop(0, rows - 2, steady)
    loop(rows - 2, rows - 1, lambda row: steady(row, first=False))
    loop(rows - 1, rows, lambda row: steady(row, middle=False, first=False))
    pipelined(written_units())
    written(rows - 1)
    clip = lax.broadcasted_iota(jnp.int32, sum_ref.shape, 1)
    weighted = jnp.sum(total[...] * table[5], keepdims=True)
    sum_ref[...] = jnp.where(clip == clip_id, jnp.broadcast_to(weighted, sum_ref.shape), 0.0)


def local(
    frames, segments, targets, in_weight, in_bias, gain_one, mid_weight, mid_bias,
    gain_two, out_weight, out_bias, head_weight, head_bias,
):
    count, rows = frames.shape[0], frames.shape[1]
    channels = in_bias.shape[0]
    width = frames.shape[2] // 3
    devices = lax.axis_size(EVERY)

    own = frames.transpose(1, 0, 2)
    previous = moved(own, POSITION, 1)
    oldest = moved(own, POSITION, 2)
    spans = (own, previous, oldest)
    low = moved(jnp.concatenate([x[rows - 3 :] for x in spans], axis=0), "band", 1)
    high = moved(jnp.concatenate([x[:3] for x in spans], axis=0), "band", -1)

    win = in_weight.transpose(2, 1, 0, 3).reshape(27, 3, channels).astype(F32)
    win = jnp.pad(win, ((0, 0), (0, SLOTS - 3), (0, 0)))
    cols = jnp.stack(
        [in_bias, gain_one, mid_bias, gain_two, out_bias, head_weight, in_bias, in_bias]
    )
    vmem = pl.BlockSpec(memory_space=pltpu.VMEM)
    features, weighted = pl.pallas_call(
        block_kernel,
        in_specs=[pl.BlockSpec(memory_space=pltpu.SMEM)] + [vmem] * 9,
        out_specs=[vmem, vmem],
        out_shape=[
            jax.ShapeDtypeStruct((rows, count, width * channels), BF16),
            jax.ShapeDtypeStruct((devices, 128), F32),
        ],
        scratch_shapes=[
            pltpu.VMEM((rows + 6, 2 * SLOTS, 3 * width), F32),
            pltpu.VMEM((9, rows + 6, 2 * SLOTS, width), F32),
            pltpu.VMEM((count * channels, 28 * SLOTS), BF16),
            pltpu.VMEM((3 * channels, 9 * channels), BF16),
            pltpu.VMEM((3 * channels, 9 * channels), BF16),
            pltpu.VMEM((rows + 4, count + 4, channels, width), BF16),
            pltpu.VMEM((rows + 2, count + 2, channels, width), BF16),
            pltpu.VMEM((rows + 4, count, channels, width), BF16),
            pltpu.VMEM((6, channels, width), F32),
            pltpu.VMEM((channels, width), F32),
            pltpu.VMEM((count, 128, width), BF16),
            pltpu.VMEM((width, width), BF16),
            pltpu.VMEM((count, width * channels), F32),
        ],
        compiler_params=pltpu.CompilerParams(vmem_limit_bytes=56 << 20),
    )(segments, own, previous, oldest, low, high, win, mid_weight, out_weight, cols)
    features = features.transpose(1, 0, 2)

    clips = targets.shape[0]
    gathered = lax.all_to_all(weighted, EVERY, 0, 0, tiled=True)
    part = jnp.sum(gathered[:, :clips], axis=0)
    labels = jnp.arange(clips, dtype=jnp.int32)
    member = (segments[:, None] == labels[None, :]).astype(F32)
    cells = jnp.sum(member, axis=0) * (count * rows * lax.axis_size("band") * width)
    scores = part / cells + head_bias[0]
    loss = jnp.mean((scores - targets) ** 2)
    return features, scores, loss


def solution(mesh):
    split = P(POSITION, "band", None)
    return jax.shard_map(
        local,
        mesh=mesh,
        in_specs=(split,) + (P(),) * 12,
        out_specs=(split, P(), P()),
        check_vma=False,
    )
```

```python
import functools

import jax
import jax.numpy as jnp
from jax import lax
from jax.experimental import pallas as pl
from jax.experimental.pallas import tpu as pltpu
from jax.sharding import PartitionSpec as P

BF16 = jnp.bfloat16
F32 = jnp.float32
POSITION = ("clip", "span")
EVERY = ("clip", "span", "band")
SLOTS = 8


def moved(block, axis, distance):
    count = lax.axis_size(axis)
    route = [(i, i + distance) for i in range(count) if 0 <= i + distance < count]
    return lax.ppermute(block, axis, route)


def shifted_sum(product, channels):
    left, middle, right = (product[k * channels : (k + 1) * channels] for k in range(3))
    lane = lax.broadcasted_iota(jnp.int32, (channels, 128), 1)
    tiles = product.shape[1] // 128
    cut = [slice(i * 128, (i + 1) * 128) for i in range(tiles)]
    left = [pltpu.roll(left[:, c], 1, 1) for c in cut]
    right = [pltpu.roll(right[:, c], 127, 1) for c in cut]
    parts = []
    for i in range(tiles):
        low = jnp.where(lane == 0, left[i - 1] if i else 0.0, left[i])
        high = jnp.where(lane == 127, right[i + 1] if i + 1 < tiles else 0.0, right[i])
        parts.append(middle[:, cut[i]] + low + high)
    return jnp.concatenate(parts, axis=1)


def rms_silu(value, half_gain, mask):
    scale = lax.rsqrt(jnp.mean(value * value, axis=0, keepdims=True) + 1e-06) * mask
    half = value * scale * half_gain
    return half + half * jnp.tanh(half)


def pipelined(units):
    waiting = []
    for start, ends in units:
        product = start()
        for end in waiting:
            end()
        waiting = [functools.partial(end, product) for end in ends]
    for end in waiting:
        end()


def prepared_kernel(
    win_ref, wmid_ref, wout_ref, cols_ref,
    flags, win, table, mid_alone, mid_both, mid_rest, out_alone, out_both, out_rest,
):
    width, channels = table.shape[2], cols_ref.shape[1]
    count = win.shape[0] // channels
    mid_parts = mid_alone, mid_both, mid_rest
    out_parts = out_alone, out_both, out_rest

    position, band = lax.axis_index(POSITION), lax.axis_index("band")
    place = lax.broadcasted_iota(jnp.int32, (1, channels), 1)

    def clip_at(index):
        chosen = jnp.where(place == index, cols_ref[6:7], 0.0)
        return jnp.sum(chosen, axis=1, keepdims=True)

    clip_id, before, older = clip_at(position), clip_at(position - 1), clip_at(position - 2)
    keep = jnp.where((position > 0) & (clip_id == before), 1.0, 0.0)
    keep_older = jnp.where((position > 1) & (older == before), keep, 0.0)
    top = jnp.where(band > 0, 1.0, 0.0)
    bottom = jnp.where(band < lax.axis_size("band") - 1, 1.0, 0.0)
    for i, flag in enumerate((keep, keep_older, top, bottom)):
        flags[i : i + 1] = jnp.broadcast_to(flag, (1, width))
    clip = lax.broadcasted_iota(jnp.int32, (1, width), 1)
    flags[4:5] = jnp.where(clip.astype(F32) == clip_id, 1.0, 0.0)
    flags[5:] = jnp.zeros((3, width), F32)

    unit = jnp.where(
        lax.broadcasted_iota(jnp.int32, (channels, channels), 0)
        == lax.broadcasted_iota(jnp.int32, (channels, channels), 1), 1.0, 0.0,
    ).astype(BF16)

    def turned(weight):
        return lax.dot_general(
            unit, weight, (((1,), (1,)), ((), ())), preferred_element_type=F32
        ).astype(BF16)

    block = 3 * channels
    begin = block // 256 * 256
    end = 3 * block // 256 * 256 + 256
    for source, (alone, both, rest) in ((wmid_ref, mid_parts), (wout_ref, out_parts)):
        for k in range(3):
            piece = jnp.concatenate(
                [
                    source[dr, dt, k * channels : (k + 1) * channels]
                    for dr in range(3) for dt in range(3)
                ],
                axis=0,
            )
            at = slice(k * channels, (k + 1) * channels)
            beside = slice(block + k * channels, block + (k + 1) * channels)
            none = jnp.zeros((end - 3 * block, channels), BF16)
            alone[at] = turned(piece[:begin])
            both[at] = turned(jnp.concatenate([piece[begin:], none], axis=0))
            none = jnp.zeros((block - begin, channels), BF16)
            both[beside] = turned(jnp.concatenate([none, piece[: end - block]], axis=0))
            rest[at] = turned(piece[end - block :])

    bias = cols_ref[:1]
    high = bias.astype(BF16).astype(F32)
    middle = (bias - high).astype(BF16).astype(F32)
    low = bias - high - middle
    bias = jnp.concatenate([high, middle, low, jnp.zeros((5, channels), F32)], axis=0)
    for t in range(count):
        piece = pltpu.roll(win_ref[...], t, 1) if t else win_ref[...]
        piece = jnp.concatenate([piece.reshape(27 * SLOTS, channels), bias], axis=0)
        win[t * channels : (t + 1) * channels] = turned(piece.astype(BF16))
    columns = jnp.transpose(cols_ref[...])
    for j in range(6):
        column = columns[:, j : j + 1] * (0.5 if j in (1, 3) else 1.0)
        table[j] = jnp.broadcast_to(column, (channels, width))


def block_kernel(
    flags, win, table, mid_alone, mid_both, mid_rest, out_alone, out_both, out_rest,
    own_ref, previous_ref, oldest_ref, low_ref, high_ref, out_hbm, sum_ref,
    out_ref, left, gathered, planes, act_one, act_two, h0_ref, total, stage, order, tiles_ref,
):
    rows, count = previous_ref.shape[0], previous_ref.shape[1]
    channels, width = table.shape[1], table.shape[2]
    pairs = width // 2
    mid_parts = mid_alone, mid_both, mid_rest
    out_parts = out_alone, out_both, out_rest
    block = 3 * channels
    begin = block // 256 * 256
    end = 3 * block // 256 * 256 + 256
    keep, keep_older, top, bottom = (flags[i : i + 1] for i in range(4))
    total[...] = jnp.zeros_like(total)

    span = 3 * pairs
    lane = lax.broadcasted_iota(jnp.int32, (span, span), 1)
    pick = lax.broadcasted_iota(jnp.int32, (span, span), 0) == 3 * (lane % pairs) + lane // pairs
    pick = jnp.where(pick, 1.0, 0.0).astype(BF16)
    sources = ((0, oldest_ref, 6, 2, 4), (2, previous_ref, 3, 0, 4), (6, own_ref, 0, 0, 2),
               (8, previous_ref, 3, 2, 4), (10, own_ref, 0, 0, 4))
    for at, source, rim, old, new in sources:
        to = slice(at, at + new - old)
        edge = 3 if source is own_ref else 0
        gathered[3 : rows + 3, to] = source[edge : rows + edge, old:new].astype(F32)
        gathered[:3, to] = low_ref[rim : rim + 3, old:new].astype(F32)
        gathered[rows + 3 :, to] = high_ref[rim : rim + 3, old:new].astype(F32)
    gathered[:, 14:] = jnp.zeros((rows + 6, 2, 3 * width), F32)
    frames = (rows + 6) * 2 * SLOTS
    flat = gathered[...].reshape(frames, 3 * width).astype(BF16)
    halves = [
        jnp.dot(flat[:, h * span : (h + 1) * span], pick, preferred_element_type=F32)
        for h in range(2)
    ]
    slot = lax.broadcasted_iota(jnp.int32, (frames, width), 0) % (2 * SLOTS)
    kept = jnp.where((slot < 6) | (slot == 8) | (slot == 9), keep, 1.0)
    kept = jnp.where(slot < 2, keep_older, kept)
    pixel = lax.broadcasted_iota(jnp.int32, (frames, width), 1)
    for c in range(3):
        plane = jnp.concatenate([h[:, c * pairs : (c + 1) * pairs] for h in halves], axis=1) * kept
        planes[c] = jnp.where(pixel == 0, 0.0, pltpu.roll(plane, 1, 1)).reshape(planes.shape[1:])
        planes[3 + c] = plane.reshape(planes.shape[1:])
        plane = jnp.where(pixel == width - 1, 0.0, pltpu.roll(plane, width - 1, 1))
        planes[6 + c] = plane.reshape(planes.shape[1:])

    part = width // 4
    row = lax.broadcasted_iota(jnp.int32, (width, width), 0)
    pixel = row % part // count * 4 + row // part
    wanted = row % count * part + pixel
    hit = lax.broadcasted_iota(jnp.int32, (width, width), 1) == wanted
    order[...] = jnp.where(hit, 1.0, 0.0).astype(BF16)
    stage[...] = jnp.zeros_like(stage)

    def row_mask(row, rim, extent):
        inside = jnp.where(row < rim, top, 1.0)
        return inside * jnp.where(row >= extent - rim, bottom, 1.0)

    def pair_units(source, parts, row, frames, done):
        alone, both, rest = parts

        def start(t):
            taps = jnp.concatenate(
                [source[row + dr, t : t + 3].reshape(block, width) for dr in range(4)], axis=0
            )
            shared = jnp.dot(both[...], taps[begin:end], preferred_element_type=F32)
            first = jnp.dot(alone[...], taps[:begin], preferred_element_type=F32)
            second = jnp.dot(rest[...], taps[end:], preferred_element_type=F32)
            return (shared[:block], first), (shared[block:], second)

        def finish(dr, t, products):
            one, other = products[dr]
            done(dr, t, one + other)

        return [
            (functools.partial(start, t), [functools.partial(finish, dr, t) for dr in range(2)])
            for t in range(frames)
        ]

    def first_units(row):
        mask = row_mask(row, 2, rows + 4)

        def end(t, at, product):
            h0 = product[at : at + channels].astype(BF16)
            if t >= 4:
                h0_ref[row, t - 4] = h0
            act = rms_silu(h0.astype(F32), table[1], mask * keep if t < 4 else mask)
            act_one[row, t] = act.astype(BF16)

        def start(half):
            taps = planes[:, pl.ds(row, 3), half * SLOTS : (half + 1) * SLOTS]
            taps = [taps.reshape(27 * SLOTS, width), jnp.ones((SLOTS, width), F32)]
            taps = jnp.concatenate(taps, axis=0).astype(BF16)
            return jnp.dot(win[...], taps, preferred_element_type=F32)

        return [
            (
                functools.partial(start, half),
                [functools.partial(end, count * half + t, t * channels) for t in range(count)],
            )
            for half in range(2)
        ]

    def middle_units(row):
        def done(dr, t, product):
            mask = row_mask(row + dr, 1, rows + 2)
            h1 = shifted_sum(product, channels) + table[2]
            act = rms_silu(h1, table[3], mask * keep if t < 2 else mask)
            act_two[row + dr, t] = act.astype(BF16)

        return pair_units(act_one, mid_parts, row, count + 2, done)

    def last_units(row):
        def done(dr, t, product):
            value = shifted_sum(product, channels) + table[4]
            value = (value + h0_ref[row + dr + 2, t].astype(F32)).astype(BF16)
            total[...] += value.astype(F32)
            stage[dr, t, :channels] = value

        return pair_units(act_two, out_parts, row, count, done)

    def written_units(dr):
        lane = lax.broadcasted_iota(jnp.int32, (128, 128), 1)

        def turned_piece(half, odd):
            sides = []
            for t in range(0, count, 2):
                one = stage[dr, t, :, half * 128 : half * 128 + 128].astype(F32)
                two = stage[dr, t + 1, :, half * 128 : half * 128 + 128].astype(F32)
                if odd:
                    one = pltpu.roll(one, part, 1)
                else:
                    two = pltpu.roll(two, part, 1)
                sides.append(jnp.transpose(jnp.where(lane < part, one, two)))
            return jnp.concatenate(sides, axis=0).astype(BF16)

        def start(half):
            both = jnp.concatenate([turned_piece(half, odd) for odd in range(2)], axis=1)
            return jnp.dot(order[...], both, preferred_element_type=F32)

        def end(half, odd, product):
            piece = 2 * half + odd
            pixels = [
                product[i * part : (i + 1) * part, odd * 128 : odd * 128 + 128] for i in range(4)
            ]
            pixels = [pltpu.roll(x, 128 - 32 * i, 1) if i else x for i, x in enumerate(pixels)]
            lane = lax.broadcasted_iota(jnp.int32, (part, 128), 1)
            for j in range(3):
                tile = jnp.where(lane < 96 - 32 * j, pixels[j], pixels[j + 1])
                for group in range(part // count):
                    at = (3 * (piece * part // count + group) + j) * 128
                    tiles_ref[dr, :, at : at + 128] = tile[group * count : (group + 1) * count]

        return [
            (functools.partial(start, half), [functools.partial(end, half, odd) for odd in range(2)])
            for half in range(2)
        ]

    def sent(row):
        pair = pl.ds(row, 2)
        return pltpu.make_async_copy(out_ref.at[pair], out_hbm.at[pair], left.at[row // 2])

    def written(row):
        for dr in range(2):
            out_ref[row + dr] = tiles_ref[dr].astype(BF16)

    def mixed(first, second):
        units = []
        for i in range(max(len(first), len(second))):
            units += first[i : i + 1] + second[i : i + 1]
        return units

    def loop(begin, end, body):
        def step(pair, carry):
            body(pair * 2)
            return carry

        lax.fori_loop(begin, end, step, 0)

    def inputs(row):
        return first_units(row) + first_units(row + 1)

    def steady(row, middle=True, first=True):
        units = mixed(
            written_units(0) + written_units(1), middle_units(row + 4) if middle else []
        )
        units += mixed(last_units(row), inputs(row + 8) if first else [])
        pipelined(units)
        written(jnp.maximum(row - 2, 0))

        @pl.when(row > 0)
        def _():
            sent(row - 2).start()

    pairs = rows // 2
    pipelined(inputs(0) + inputs(2))
    loop(0, 2, lambda row: pipelined(mixed(middle_units(row), inputs(row + 4))))
    loop(0, pairs - 2, steady)
    loop(pairs - 2, pairs - 1, lambda row: steady(row, first=False))
    loop(pairs - 1, pairs, lambda row: steady(row, middle=False, first=False))
    pipelined(written_units(0) + written_units(1))
    written(rows - 2)
    sent(rows - 2).start()
    weighted = jnp.sum(total[...] * table[5], keepdims=True)
    sum_ref[...] = jnp.broadcast_to(weighted * flags[4:5, :128], sum_ref.shape)
    for pair in range(pairs):
        sent(2 * pair).wait()


def local(
    frames, segments, targets, in_weight, in_bias, gain_one, mid_weight, mid_bias,
    gain_two, out_weight, out_bias, head_weight, head_bias,
):
    count, rows = frames.shape[0], frames.shape[1]
    channels = in_bias.shape[0]
    width = frames.shape[2] // 3
    devices = lax.axis_size(EVERY)

    own = frames.transpose(1, 0, 2)
    previous = moved(own, POSITION, 1)
    oldest = moved(own, POSITION, 2)
    padded = lax.optimization_barrier(jnp.pad(own, ((3, 3), (0, 0), (0, 0))))
    spans = (padded[3 : rows + 3], previous, oldest)
    low = moved(jnp.concatenate([x[rows - 3 :] for x in spans], axis=0), "band", 1)
    high = moved(jnp.concatenate([x[:3] for x in spans], axis=0), "band", -1)

    win = in_weight.transpose(2, 1, 0, 3).reshape(27, 3, channels).astype(F32)
    win = jnp.pad(win, ((0, 0), (0, SLOTS - 3), (0, 0)))
    clip_row = jnp.pad(segments.astype(F32), (0, channels - segments.shape[0]))
    cols = jnp.stack(
        [in_bias, gain_one, mid_bias, gain_two, out_bias, head_weight, clip_row, in_bias]
    )
    block = 3 * channels
    begin, end = block // 256 * 256, 3 * block // 256 * 256 + 256
    parts = [(block, begin), (2 * block, end - begin), (block, 4 * block - end)] * 2
    vmem = pl.BlockSpec(memory_space=pltpu.VMEM)
    prepared = pl.pallas_call(
        prepared_kernel,
        in_specs=[vmem] * 4,
        out_specs=[vmem] * 9,
        out_shape=[
            jax.ShapeDtypeStruct((8, width), F32),
            jax.ShapeDtypeStruct((count * channels, 28 * SLOTS), BF16),
            jax.ShapeDtypeStruct((6, channels, width), F32),
        ] + [jax.ShapeDtypeStruct(shape, BF16) for shape in parts],
        compiler_params=pltpu.CompilerParams(vmem_limit_bytes=12 << 20),
        cost_estimate=pl.CostEstimate(flops=10**9, bytes_accessed=6 * 10**6, transcendentals=0),
    )(win, mid_weight.swapaxes(0, 1), out_weight.swapaxes(0, 1), cols)
    features, weighted = pl.pallas_call(
        block_kernel,
        in_specs=[vmem] * 14,
        out_specs=[pl.BlockSpec(memory_space=pltpu.HBM), vmem],
        out_shape=[
            jax.ShapeDtypeStruct((rows, count, width * channels), BF16),
            jax.ShapeDtypeStruct((devices, 128), F32),
        ],
        scratch_shapes=[
            pltpu.VMEM((rows, count, width * channels), BF16),
            pltpu.SemaphoreType.DMA((rows // 2,)),
            pltpu.VMEM((rows + 6, 2 * SLOTS, 3 * width), F32),
            pltpu.VMEM((9, rows + 6, 2 * SLOTS, width), F32),
            pltpu.VMEM((rows + 4, count + 4, channels, width), BF16),
            pltpu.VMEM((rows + 2, count + 2, channels, width), BF16),
            pltpu.VMEM((rows + 4, count, channels, width), BF16),
            pltpu.VMEM((channels, width), F32),
            pltpu.VMEM((2, count, 128, width), BF16),
            pltpu.VMEM((width, width), BF16),
            pltpu.VMEM((2, count, width * channels), F32),
        ],
        compiler_params=pltpu.CompilerParams(vmem_limit_bytes=32 << 20),
    )(*prepared, padded, previous, oldest, low, high)
    features = features.transpose(1, 0, 2)

    clips = targets.shape[0]
    gathered = lax.all_to_all(weighted, EVERY, 0, 0, tiled=True)
    part = jnp.sum(gathered[:, :clips], axis=0)
    labels = jnp.arange(clips, dtype=jnp.int32)
    member = (segments[:, None] == labels[None, :]).astype(F32)
    cells = jnp.sum(member, axis=0) * (count * rows * lax.axis_size("band") * width)
    scores = part / cells + head_bias[0]
    loss = jnp.mean((scores - targets) ** 2)
    return features, scores, loss


def solution(mesh):
    split = P(POSITION, "band", None)
    return jax.shard_map(
        local,
        mesh=mesh,
        in_specs=(split,) + (P(),) * 12,
        out_specs=(split, P(), P()),
        check_vma=False,
    )
```

```python
import functools

import jax
import jax.numpy as jnp
from jax import lax
from jax.experimental import pallas as pl
from jax.experimental.pallas import tpu as pltpu
from jax.sharding import PartitionSpec as P

BF16 = jnp.bfloat16
F32 = jnp.float32
POSITION = ("clip", "span")
EVERY = ("clip", "span", "band")
SLOTS = 8


def moved(block, axis, distance):
    count = lax.axis_size(axis)
    route = [(i, i + distance) for i in range(count) if 0 <= i + distance < count]
    return lax.ppermute(block, axis, route)


def shifted_sum(product, channels):
    left, middle, right = (product[k * channels : (k + 1) * channels] for k in range(3))
    lane = lax.broadcasted_iota(jnp.int32, (channels, 128), 1)
    tiles = product.shape[1] // 128
    cut = [slice(i * 128, (i + 1) * 128) for i in range(tiles)]
    left = [pltpu.roll(left[:, c], 1, 1) for c in cut]
    right = [pltpu.roll(right[:, c], 127, 1) for c in cut]
    parts = []
    for i in range(tiles):
        low = jnp.where(lane == 0, left[i - 1] if i else 0.0, left[i])
        high = jnp.where(lane == 127, right[i + 1] if i + 1 < tiles else 0.0, right[i])
        parts.append(middle[:, cut[i]] + low + high)
    return jnp.concatenate(parts, axis=1)


def rms_silu(value, half_gain, mask):
    scale = lax.rsqrt(jnp.mean(value * value, axis=0, keepdims=True) + 1e-06) * mask
    half = value * scale * half_gain
    return half + half * jnp.tanh(half)


def pipelined(units):
    waiting = []
    for start, ends in units:
        product = start()
        for end in waiting:
            end()
        waiting = [functools.partial(end, product) for end in ends]
    for end in waiting:
        end()


def prepared_kernel(
    win_ref, wmid_ref, wout_ref, cols_ref,
    flags, win, table, mid_alone, mid_both, mid_rest, out_alone, out_both, out_rest,
):
    width, channels = table.shape[2], cols_ref.shape[1]
    count = win.shape[0] // channels
    mid_parts = mid_alone, mid_both, mid_rest
    out_parts = out_alone, out_both, out_rest

    position, band = lax.axis_index(POSITION), lax.axis_index("band")
    place = lax.broadcasted_iota(jnp.int32, (1, channels), 1)

    def clip_at(index):
        chosen = jnp.where(place == index, cols_ref[6:7], 0.0)
        return jnp.sum(chosen, axis=1, keepdims=True)

    clip_id, before, older = clip_at(position), clip_at(position - 1), clip_at(position - 2)
    keep = jnp.where((position > 0) & (clip_id == before), 1.0, 0.0)
    keep_older = jnp.where((position > 1) & (older == before), keep, 0.0)
    top = jnp.where(band > 0, 1.0, 0.0)
    bottom = jnp.where(band < lax.axis_size("band") - 1, 1.0, 0.0)
    for i, flag in enumerate((keep, keep_older, top, bottom)):
        flags[i : i + 1] = jnp.broadcast_to(flag, (1, width))
    clip = lax.broadcasted_iota(jnp.int32, (1, width), 1)
    flags[4:5] = jnp.where(clip.astype(F32) == clip_id, 1.0, 0.0)
    flags[5:] = jnp.zeros((3, width), F32)

    unit = jnp.where(
        lax.broadcasted_iota(jnp.int32, (channels, channels), 0)
        == lax.broadcasted_iota(jnp.int32, (channels, channels), 1), 1.0, 0.0,
    ).astype(BF16)

    def turned(weight):
        return lax.dot_general(
            unit, weight, (((1,), (1,)), ((), ())), preferred_element_type=F32
        ).astype(BF16)

    block = 3 * channels
    begin = block // 256 * 256
    end = 3 * block // 256 * 256 + 256
    for source, (alone, both, rest) in ((wmid_ref, mid_parts), (wout_ref, out_parts)):
        for k in range(3):
            piece = jnp.concatenate(
                [
                    source[dr, dt, k * channels : (k + 1) * channels]
                    for dr in range(3) for dt in range(3)
                ],
                axis=0,
            )
            at = slice(k * channels, (k + 1) * channels)
            beside = slice(block + k * channels, block + (k + 1) * channels)
            none = jnp.zeros((end - 3 * block, channels), BF16)
            alone[at] = turned(piece[:begin])
            both[at] = turned(jnp.concatenate([piece[begin:], none], axis=0))
            none = jnp.zeros((block - begin, channels), BF16)
            both[beside] = turned(jnp.concatenate([none, piece[: end - block]], axis=0))
            rest[at] = turned(piece[end - block :])

    bias = cols_ref[:1]
    high = bias.astype(BF16).astype(F32)
    middle = (bias - high).astype(BF16).astype(F32)
    low = bias - high - middle
    bias = jnp.concatenate([high, middle, low, jnp.zeros((5, channels), F32)], axis=0)
    for t in range(count):
        piece = pltpu.roll(win_ref[...], t, 1) if t else win_ref[...]
        piece = jnp.concatenate([piece.reshape(27 * SLOTS, channels), bias], axis=0)
        win[t * channels : (t + 1) * channels] = turned(piece.astype(BF16))
    columns = jnp.transpose(cols_ref[...])
    for j in range(6):
        column = columns[:, j : j + 1] * (0.5 if j in (1, 3) else 1.0)
        table[j] = jnp.broadcast_to(column, (channels, width))


def block_kernel(
    flags, win, table, mid_alone, mid_both, mid_rest, out_alone, out_both, out_rest,
    own_ref, previous_ref, oldest_ref, low_ref, high_ref, out_hbm, sum_ref,
    out_ref, left, gathered, planes, act_one, act_two, h0_ref, total, stage, order, tiles_ref,
):
    rows, count = previous_ref.shape[0], previous_ref.shape[1]
    channels, width = table.shape[1], table.shape[2]
    pairs = width // 2
    mid_parts = mid_alone, mid_both, mid_rest
    out_parts = out_alone, out_both, out_rest
    block = 3 * channels
    begin = block // 256 * 256
    end = 3 * block // 256 * 256 + 256
    keep, keep_older, top, bottom = (flags[i : i + 1] for i in range(4))
    total[...] = jnp.zeros_like(total)

    span = 3 * pairs
    lane = lax.broadcasted_iota(jnp.int32, (span, span), 1)
    pick = lax.broadcasted_iota(jnp.int32, (span, span), 0) == 3 * (lane % pairs) + lane // pairs
    pick = jnp.where(pick, 1.0, 0.0).astype(BF16)
    sources = ((0, oldest_ref, 6, 2, 4), (2, previous_ref, 3, 0, 4), (6, own_ref, 0, 0, 2),
               (8, previous_ref, 3, 2, 4), (10, own_ref, 0, 0, 4))
    for at, source, rim, old, new in sources:
        to = slice(at, at + new - old)
        edge = 3 if source is own_ref else 0
        gathered[3 : rows + 3, to] = source[edge : rows + edge, old:new].astype(F32)
        gathered[:3, to] = low_ref[rim : rim + 3, old:new].astype(F32)
        gathered[rows + 3 :, to] = high_ref[rim : rim + 3, old:new].astype(F32)
    gathered[:, 14:] = jnp.zeros((rows + 6, 2, 3 * width), F32)
    frames = (rows + 6) * 2 * SLOTS
    flat = gathered[...].reshape(frames, 3 * width).astype(BF16)
    halves = [
        jnp.dot(flat[:, h * span : (h + 1) * span], pick, preferred_element_type=F32)
        for h in range(2)
    ]
    slot = lax.broadcasted_iota(jnp.int32, (frames, width), 0) % (2 * SLOTS)
    kept = jnp.where((slot < 6) | (slot == 8) | (slot == 9), keep, 1.0)
    kept = jnp.where(slot < 2, keep_older, kept)
    pixel = lax.broadcasted_iota(jnp.int32, (frames, width), 1)
    for c in range(3):
        plane = jnp.concatenate([h[:, c * pairs : (c + 1) * pairs] for h in halves], axis=1) * kept
        planes[c] = jnp.where(pixel == 0, 0.0, pltpu.roll(plane, 1, 1)).reshape(planes.shape[1:])
        planes[3 + c] = plane.reshape(planes.shape[1:])
        plane = jnp.where(pixel == width - 1, 0.0, pltpu.roll(plane, width - 1, 1))
        planes[6 + c] = plane.reshape(planes.shape[1:])

    part = width // 4
    row = lax.broadcasted_iota(jnp.int32, (width, width), 0)
    pixel = row % part // count * 4 + row // part
    wanted = row % count * part + pixel
    hit = lax.broadcasted_iota(jnp.int32, (width, width), 1) == wanted
    order[...] = jnp.where(hit, 1.0, 0.0).astype(BF16)
    stage[...] = jnp.zeros_like(stage)

    def row_mask(row, rim, extent):
        inside = jnp.where(row < rim, top, 1.0)
        return inside * jnp.where(row >= extent - rim, bottom, 1.0)

    def pair_units(source, parts, row, frames, done):
        alone, both, rest = parts

        def start(t):
            taps = jnp.concatenate(
                [source[row + dr, t : t + 3].reshape(block, width) for dr in range(4)], axis=0
            )
            shared = jnp.dot(both[...], taps[begin:end], preferred_element_type=F32)
            first = jnp.dot(alone[...], taps[:begin], preferred_element_type=F32)
            second = jnp.dot(rest[...], taps[end:], preferred_element_type=F32)
            return (shared[:block], first), (shared[block:], second)

        def finish(dr, t, products):
            one, other = products[dr]
            done(dr, t, one + other)

        return [
            (functools.partial(start, t), [functools.partial(finish, dr, t) for dr in range(2)])
            for t in range(frames)
        ]

    def first_units(row):
        mask = row_mask(row, 2, rows + 4)

        def end(t, at, product):
            h0 = product[at : at + channels].astype(BF16)
            if t >= 4:
                h0_ref[row, t - 4] = h0
            act = rms_silu(h0.astype(F32), table[1], mask * keep if t < 4 else mask)
            act_one[row, t] = act.astype(BF16)

        def start(half):
            taps = planes[:, pl.ds(row, 3), half * SLOTS : (half + 1) * SLOTS]
            taps = [taps.reshape(27 * SLOTS, width), jnp.ones((SLOTS, width), F32)]
            taps = jnp.concatenate(taps, axis=0).astype(BF16)
            return jnp.dot(win[...], taps, preferred_element_type=F32)

        return [
            (
                functools.partial(start, half),
                [functools.partial(end, count * half + t, t * channels) for t in range(count)],
            )
            for half in range(2)
        ]

    def middle_units(row):
        def done(dr, t, product):
            mask = row_mask(row + dr, 1, rows + 2)
            h1 = shifted_sum(product, channels) + table[2]
            act = rms_silu(h1, table[3], mask * keep if t < 2 else mask)
            act_two[row + dr, t] = act.astype(BF16)

        return pair_units(act_one, mid_parts, row, count + 2, done)

    def last_units(row):
        def done(dr, t, product):
            value = shifted_sum(product, channels) + table[4]
            value = (value + h0_ref[row + dr + 2, t].astype(F32)).astype(BF16)
            total[...] += value.astype(F32)
            stage[dr, t, :channels] = value

        return pair_units(act_two, out_parts, row, count, done)

    def written_units(dr):
        lane = lax.broadcasted_iota(jnp.int32, (128, 128), 1)

        def turned_piece(half, odd):
            sides = []
            for t in range(0, count, 2):
                one = stage[dr, t, :, half * 128 : half * 128 + 128].astype(F32)
                two = stage[dr, t + 1, :, half * 128 : half * 128 + 128].astype(F32)
                if odd:
                    one = pltpu.roll(one, part, 1)
                else:
                    two = pltpu.roll(two, part, 1)
                sides.append(jnp.transpose(jnp.where(lane < part, one, two)))
            return jnp.concatenate(sides, axis=0).astype(BF16)

        def start(half):
            both = jnp.concatenate([turned_piece(half, odd) for odd in range(2)], axis=1)
            return jnp.dot(order[...], both, preferred_element_type=F32)

        def end(half, odd, product):
            piece = 2 * half + odd
            pixels = [
                product[i * part : (i + 1) * part, odd * 128 : odd * 128 + 128] for i in range(4)
            ]
            pixels = [pltpu.roll(x, 128 - 32 * i, 1) if i else x for i, x in enumerate(pixels)]
            lane = lax.broadcasted_iota(jnp.int32, (part, 128), 1)
            for j in range(3):
                tile = jnp.where(lane < 96 - 32 * j, pixels[j], pixels[j + 1])
                for group in range(part // count):
                    at = (3 * (piece * part // count + group) + j) * 128
                    tiles_ref[dr, :, at : at + 128] = tile[group * count : (group + 1) * count]

        return [
            (functools.partial(start, half), [functools.partial(end, half, odd) for odd in range(2)])
            for half in range(2)
        ]

    def sent(row):
        pair = pl.ds(row, 2)
        return pltpu.make_async_copy(out_ref.at[pair], out_hbm.at[pair], left.at[row // 2])

    def written(row):
        for dr in range(2):
            out_ref[row + dr] = tiles_ref[dr].astype(BF16)

    def mixed(first, second):
        units = []
        for i in range(max(len(first), len(second))):
            units += first[i : i + 1] + second[i : i + 1]
        return units

    def loop(begin, end, body):
        for pair in range(begin, end):
            body(pair * 2)

    def inputs(row):
        return first_units(row) + first_units(row + 1)

    def steady(row, middle=True, first=True):
        units = mixed(
            written_units(0) + written_units(1) if row else [],
            middle_units(row + 4) if middle else [],
        )
        units += mixed(last_units(row), inputs(row + 8) if first else [])
        pipelined(units)
        if row:
            written(row - 2)
            sent(row - 2).start()

    pairs = rows // 2
    pipelined(inputs(0) + inputs(2))
    loop(0, 2, lambda row: pipelined(mixed(middle_units(row), inputs(row + 4))))
    loop(0, pairs - 2, steady)
    loop(pairs - 2, pairs - 1, lambda row: steady(row, first=False))
    loop(pairs - 1, pairs, lambda row: steady(row, middle=False, first=False))
    pipelined(written_units(0) + written_units(1))
    written(rows - 2)
    sent(rows - 2).start()
    weighted = jnp.sum(total[...] * table[5], keepdims=True)
    sum_ref[...] = jnp.broadcast_to(weighted * flags[4:5, :128], sum_ref.shape)
    for pair in range(pairs):
        sent(2 * pair).wait()


def local(
    frames, segments, targets, in_weight, in_bias, gain_one, mid_weight, mid_bias,
    gain_two, out_weight, out_bias, head_weight, head_bias,
):
    count, rows = frames.shape[0], frames.shape[1]
    channels = in_bias.shape[0]
    width = frames.shape[2] // 3
    devices = lax.axis_size(EVERY)

    own = frames.transpose(1, 0, 2)
    previous = moved(own, POSITION, 1)
    oldest = moved(own, POSITION, 2)
    padded = lax.optimization_barrier(jnp.pad(own, ((3, 3), (0, 0), (0, 0))))
    spans = (padded[3 : rows + 3], previous, oldest)
    low = moved(jnp.concatenate([x[rows - 3 :] for x in spans], axis=0), "band", 1)
    high = moved(jnp.concatenate([x[:3] for x in spans], axis=0), "band", -1)

    win = in_weight.transpose(2, 1, 0, 3).reshape(27, 3, channels).astype(F32)
    win = jnp.pad(win, ((0, 0), (0, SLOTS - 3), (0, 0)))
    clip_row = jnp.pad(segments.astype(F32), (0, channels - segments.shape[0]))
    cols = jnp.stack(
        [in_bias, gain_one, mid_bias, gain_two, out_bias, head_weight, clip_row, in_bias]
    )
    block = 3 * channels
    begin, end = block // 256 * 256, 3 * block // 256 * 256 + 256
    parts = [(block, begin), (2 * block, end - begin), (block, 4 * block - end)] * 2
    vmem = pl.BlockSpec(memory_space=pltpu.VMEM)
    prepared = pl.pallas_call(
        prepared_kernel,
        in_specs=[vmem] * 4,
        out_specs=[vmem] * 9,
        out_shape=[
            jax.ShapeDtypeStruct((8, width), F32),
            jax.ShapeDtypeStruct((count * channels, 28 * SLOTS), BF16),
            jax.ShapeDtypeStruct((6, channels, width), F32),
        ] + [jax.ShapeDtypeStruct(shape, BF16) for shape in parts],
        compiler_params=pltpu.CompilerParams(vmem_limit_bytes=12 << 20),
        cost_estimate=pl.CostEstimate(flops=10**9, bytes_accessed=6 * 10**6, transcendentals=0),
    )(win, mid_weight.swapaxes(0, 1), out_weight.swapaxes(0, 1), cols)
    features, weighted = pl.pallas_call(
        block_kernel,
        in_specs=[vmem] * 14,
        out_specs=[pl.BlockSpec(memory_space=pltpu.HBM), vmem],
        out_shape=[
            jax.ShapeDtypeStruct((rows, count, width * channels), BF16),
            jax.ShapeDtypeStruct((devices, 128), F32),
        ],
        scratch_shapes=[
            pltpu.VMEM((rows, count, width * channels), BF16),
            pltpu.SemaphoreType.DMA((rows // 2,)),
            pltpu.VMEM((rows + 6, 2 * SLOTS, 3 * width), F32),
            pltpu.VMEM((9, rows + 6, 2 * SLOTS, width), F32),
            pltpu.VMEM((rows + 4, count + 4, channels, width), BF16),
            pltpu.VMEM((rows + 2, count + 2, channels, width), BF16),
            pltpu.VMEM((rows + 4, count, channels, width), BF16),
            pltpu.VMEM((channels, width), F32),
            pltpu.VMEM((2, count, 128, width), BF16),
            pltpu.VMEM((width, width), BF16),
            pltpu.VMEM((2, count, width * channels), F32),
        ],
        compiler_params=pltpu.CompilerParams(vmem_limit_bytes=32 << 20),
    )(*prepared, padded, previous, oldest, low, high)
    features = features.transpose(1, 0, 2)

    clips = targets.shape[0]
    gathered = lax.all_to_all(weighted, EVERY, 0, 0, tiled=True)
    part = jnp.sum(gathered[:, :clips], axis=0)
    labels = jnp.arange(clips, dtype=jnp.int32)
    member = (segments[:, None] == labels[None, :]).astype(F32)
    cells = jnp.sum(member, axis=0) * (count * rows * lax.axis_size("band") * width)
    scores = part / cells + head_bias[0]
    loss = jnp.mean((scores - targets) ** 2)
    return features, scores, loss


def solution(mesh):
    split = P(POSITION, "band", None)
    return jax.shard_map(
        local,
        mesh=mesh,
        in_specs=(split,) + (P(),) * 12,
        out_specs=(split, P(), P()),
        check_vma=False,
    )
```

```python
import functools

import jax
import jax.numpy as jnp
from jax import lax
from jax.experimental import pallas as pl
from jax.experimental.pallas import tpu as pltpu
from jax.sharding import PartitionSpec as P

BF16 = jnp.bfloat16
F32 = jnp.float32
POSITION = ("clip", "span")
EVERY = ("clip", "span", "band")
HANDED = 160
SLOTS = 8


def moved(block, axis, distance):
    count = lax.axis_size(axis)
    route = [(i, i + distance) for i in range(count) if 0 <= i + distance < count]
    return lax.ppermute(block, axis, route)


def shifted_sum(product, channels):
    left, middle, right = (product[k * channels : (k + 1) * channels] for k in range(3))
    lane = lax.broadcasted_iota(jnp.int32, (channels, 128), 1)
    tiles = product.shape[1] // 128
    cut = [slice(i * 128, (i + 1) * 128) for i in range(tiles)]
    left = [pltpu.roll(left[:, c], 1, 1) for c in cut]
    right = [pltpu.roll(right[:, c], 127, 1) for c in cut]
    parts = []
    for i in range(tiles):
        low = jnp.where(lane == 0, left[i - 1] if i else 0.0, left[i])
        high = jnp.where(lane == 127, right[i + 1] if i + 1 < tiles else 0.0, right[i])
        parts.append(middle[:, cut[i]] + low + high)
    return jnp.concatenate(parts, axis=1)


def rms_silu(value, half_gain, mask):
    scale = lax.rsqrt(jnp.mean(value * value, axis=0, keepdims=True) + 1e-06) * mask
    half = value * scale * half_gain
    return half + half * jnp.tanh(half)


def pipelined(units):
    waiting = []
    for start, ends in units:
        product = start()
        for end in waiting:
            end()
        waiting = [functools.partial(end, product) for end in ends]
    for end in waiting:
        end()


def split_three(row, channels):
    high = row.astype(BF16).astype(F32)
    middle = (row - high).astype(BF16).astype(F32)
    low = row - high - middle
    rows = jnp.concatenate([high, middle, low, jnp.zeros((5, channels), F32)], axis=0)
    return rows.astype(BF16)


def prepared_kernel(
    win_ref, wmid_ref, wout_ref, cols_ref,
    flags, win, table, coefs, mid_alone, mid_both, mid_rest, out_alone, out_both, out_rest,
):
    width, channels = table.shape[2], cols_ref.shape[1]
    count = win.shape[0] // channels
    mid_parts = mid_alone, mid_both, mid_rest
    out_parts = out_alone, out_both, out_rest

    position, band = lax.axis_index(POSITION), lax.axis_index("band")
    place = lax.broadcasted_iota(jnp.int32, (1, channels), 1)

    def clip_at(index):
        chosen = jnp.where(place == index, cols_ref[6:7], 0.0)
        return jnp.sum(chosen, axis=1, keepdims=True)

    clip_id, before, older = clip_at(position), clip_at(position - 1), clip_at(position - 2)
    keep = jnp.where((position > 0) & (clip_id == before), 1.0, 0.0)
    keep_older = jnp.where((position > 1) & (older == before), keep, 0.0)
    top = jnp.where(band > 0, 1.0, 0.0)
    bottom = jnp.where(band < lax.axis_size("band") - 1, 1.0, 0.0)
    for i, flag in enumerate((keep, keep_older, top, bottom)):
        flags[i : i + 1] = jnp.broadcast_to(flag, (1, width))
    clip = lax.broadcasted_iota(jnp.int32, (1, width), 1)
    flags[4:5] = jnp.where(clip.astype(F32) == clip_id, 1.0, 0.0)
    flags[5:] = jnp.zeros((3, width), F32)

    unit = jnp.where(
        lax.broadcasted_iota(jnp.int32, (channels, channels), 0)
        == lax.broadcasted_iota(jnp.int32, (channels, channels), 1), 1.0, 0.0,
    ).astype(BF16)

    def turned(weight):
        return lax.dot_general(
            unit, weight, (((1,), (1,)), ((), ())), preferred_element_type=F32
        ).astype(BF16)

    block = 3 * channels
    begin = block // 256 * 256
    end = 3 * block // 256 * 256 + 256
    head = split_three(cols_ref[5:6], channels)
    for source, (alone, both, rest) in ((wmid_ref, mid_parts), (wout_ref, out_parts)):
        for k in range(3):
            piece = jnp.concatenate(
                [
                    source[dr, dt, k * channels : (k + 1) * channels]
                    for dr in range(3) for dt in range(3)
                ],
                axis=0,
            )
            if source is wout_ref:
                toward = lax.dot_general(
                    piece, head, (((1,), (1,)), ((), ())), preferred_element_type=F32
                )
                toward = jnp.sum(toward, axis=1, keepdims=True)
                coefs[k] = jnp.broadcast_to(toward, (3 * block, 128))
            at = slice(k * channels, (k + 1) * channels)
            beside = slice(block + k * channels, block + (k + 1) * channels)
            none = jnp.zeros((end - 3 * block, channels), BF16)
            alone[at] = turned(piece[:begin])
            both[at] = turned(jnp.concatenate([piece[begin:], none], axis=0))
            none = jnp.zeros((block - begin, channels), BF16)
            both[beside] = turned(jnp.concatenate([none, piece[: end - block]], axis=0))
            rest[at] = turned(piece[end - block :])

    bias = split_three(cols_ref[:1], channels).astype(F32)
    for t in range(count):
        piece = pltpu.roll(win_ref[...], t, 1) if t else win_ref[...]
        piece = jnp.concatenate([piece.reshape(27 * SLOTS, channels), bias], axis=0)
        win[t * channels : (t + 1) * channels] = turned(piece.astype(BF16))
    columns = jnp.transpose(cols_ref[...])
    for j in range(6):
        column = columns[:, j : j + 1] * (0.5 if j in (1, 3) else 1.0)
        table[j] = jnp.broadcast_to(column, (channels, width))


def order_of_pixels(order, stage, width, count):
    part = width // 4
    row = lax.broadcasted_iota(jnp.int32, (width, width), 0)
    pixel = row % part // count * 4 + row // part
    wanted = row % count * part + pixel
    hit = lax.broadcasted_iota(jnp.int32, (width, width), 1) == wanted
    order[...] = jnp.where(hit, 1.0, 0.0).astype(BF16)
    stage[...] = jnp.zeros_like(stage)


def pair_units(source, parts, row, frames, done):
    channels, width = source.shape[2], source.shape[3]
    block = 3 * channels
    begin = block // 256 * 256
    end = 3 * block // 256 * 256 + 256
    alone, both, rest = parts

    def start(t):
        taps = jnp.concatenate(
            [source[row + dr, t : t + 3].reshape(block, width) for dr in range(4)], axis=0
        )
        shared = jnp.dot(both[...], taps[begin:end], preferred_element_type=F32)
        first = jnp.dot(alone[...], taps[:begin], preferred_element_type=F32)
        second = jnp.dot(rest[...], taps[end:], preferred_element_type=F32)
        return (shared[:block], first), (shared[block:], second)

    def finish(dr, t, products):
        one, other = products[dr]
        done(dr, t, one + other)

    return [
        (functools.partial(start, t), [functools.partial(finish, dr, t) for dr in range(2)])
        for t in range(frames)
    ]


def mixed(first, second):
    units = []
    for i in range(max(len(first), len(second))):
        units += first[i : i + 1] + second[i : i + 1]
    return units


def writer(
    act_two, h0_ref, lag, out_parts, table, stage, order, tiles_ref, out_ref, out_hbm, left, shift
):
    channels, width = act_two.shape[2], act_two.shape[3]
    count, part = out_ref.shape[1], width // 4

    def last_units(row):
        def done(dr, t, product):
            value = shifted_sum(product, channels) + table[4]
            value = (value + h0_ref[row + dr + lag, t].astype(F32)).astype(BF16)
            stage[dr, t, :channels] = value

        return pair_units(act_two, out_parts, row, count, done)

    def written_units(dr):
        lane = lax.broadcasted_iota(jnp.int32, (128, 128), 1)

        def turned_piece(half, odd):
            sides = []
            for t in range(0, count, 2):
                one = stage[dr, t, :, half * 128 : half * 128 + 128].astype(F32)
                two = stage[dr, t + 1, :, half * 128 : half * 128 + 128].astype(F32)
                if odd:
                    one = pltpu.roll(one, part, 1)
                else:
                    two = pltpu.roll(two, part, 1)
                sides.append(jnp.transpose(jnp.where(lane < part, one, two)))
            return jnp.concatenate(sides, axis=0).astype(BF16)

        def start(half):
            both = jnp.concatenate([turned_piece(half, odd) for odd in range(2)], axis=1)
            return jnp.dot(order[...], both, preferred_element_type=F32)

        def end(half, odd, product):
            piece = 2 * half + odd
            pixels = [
                product[i * part : (i + 1) * part, odd * 128 : odd * 128 + 128] for i in range(4)
            ]
            pixels = [pltpu.roll(x, 128 - 32 * i, 1) if i else x for i, x in enumerate(pixels)]
            lane = lax.broadcasted_iota(jnp.int32, (part, 128), 1)
            for j in range(3):
                tile = jnp.where(lane < 96 - 32 * j, pixels[j], pixels[j + 1])
                for group in range(part // count):
                    at = (3 * (piece * part // count + group) + j) * 128
                    tiles_ref[dr, :, at : at + 128] = tile[group * count : (group + 1) * count]

        return [
            (functools.partial(start, half), [functools.partial(end, half, odd) for odd in range(2)])
            for half in range(2)
        ]

    def sent(row):
        here, there = pl.ds(row, 2), pl.ds(row + shift, 2)
        return pltpu.make_async_copy(out_ref.at[here], out_hbm.at[there], left.at[row // 2])

    def written(row):
        for dr in range(2):
            out_ref[row + dr] = tiles_ref[dr].astype(BF16)

    return last_units, written_units, written, sent


def block_kernel(
    flags, win, table, coefs, mid_alone, mid_both, mid_rest, out_alone, out_both, out_rest,
    own_ref, previous_ref, oldest_ref, low_ref, high_ref, out_hbm, sum_ref, rest_hbm,
    rest, handed, out_ref, left, gathered, planes, act_one, act_two, h0_ref, total, sums, stage, order, tiles_ref,
):
    rows, count = previous_ref.shape[0], previous_ref.shape[1]
    channels, width = table.shape[1], table.shape[2]
    pairs = width // 2
    mid_parts = mid_alone, mid_both, mid_rest
    out_parts = out_alone, out_both, out_rest
    block = 3 * channels
    begin = block // 256 * 256
    end = 3 * block // 256 * 256 + 256
    early = out_ref.shape[0]
    late = rows - early

    def handing(row):
        pair = pl.ds(row, 2), pl.ds(0, count if row >= late + 2 else count + 2)
        return pltpu.make_async_copy(rest.at[pair], rest_hbm.at[pair], handed.at[row // 2])

    keep, keep_older, top, bottom = (flags[i : i + 1] for i in range(4))
    total[...] = jnp.zeros_like(total)

    span = 3 * pairs
    lane = lax.broadcasted_iota(jnp.int32, (span, span), 1)
    pick = lax.broadcasted_iota(jnp.int32, (span, span), 0) == 3 * (lane % pairs) + lane // pairs
    pick = jnp.where(pick, 1.0, 0.0).astype(BF16)
    sources = ((0, oldest_ref, 6, 2, 4), (2, previous_ref, 3, 0, 4), (6, own_ref, 0, 0, 2),
               (8, previous_ref, 3, 2, 4), (10, own_ref, 0, 0, 4))
    for at, source, rim, old, new in sources:
        to = slice(at, at + new - old)
        edge = 3 if source is own_ref else 0
        gathered[3 : rows + 3, to] = source[edge : rows + edge, old:new].astype(F32)
        gathered[:3, to] = low_ref[rim : rim + 3, old:new].astype(F32)
        gathered[rows + 3 :, to] = high_ref[rim : rim + 3, old:new].astype(F32)
    gathered[:, 14:] = jnp.zeros((rows + 6, 2, 3 * width), F32)
    frames = (rows + 6) * 2 * SLOTS
    flat = gathered[...].reshape(frames, 3 * width).astype(BF16)
    halves = [
        jnp.dot(flat[:, h * span : (h + 1) * span], pick, preferred_element_type=F32)
        for h in range(2)
    ]
    slot = lax.broadcasted_iota(jnp.int32, (frames, width), 0) % (2 * SLOTS)
    kept = jnp.where((slot < 6) | (slot == 8) | (slot == 9), keep, 1.0)
    kept = jnp.where(slot < 2, keep_older, kept)
    pixel = lax.broadcasted_iota(jnp.int32, (frames, width), 1)
    for c in range(3):
        plane = jnp.concatenate([h[:, c * pairs : (c + 1) * pairs] for h in halves], axis=1) * kept
        planes[c] = jnp.where(pixel == 0, 0.0, pltpu.roll(plane, 1, 1)).reshape(planes.shape[1:])
        planes[3 + c] = plane.reshape(planes.shape[1:])
        plane = jnp.where(pixel == width - 1, 0.0, pltpu.roll(plane, width - 1, 1))
        planes[6 + c] = plane.reshape(planes.shape[1:])

    order_of_pixels(order, stage, width, count)
    sums[...] = jnp.zeros_like(sums)

    def row_mask(row, rim, extent):
        inside = jnp.where(row < rim, top, 1.0)
        return inside * jnp.where(row >= extent - rim, bottom, 1.0)

    def first_units(row):
        mask = row_mask(row, 2, rows + 4)

        def end(t, at, product):
            h0 = product[at : at + channels].astype(BF16)
            if t >= 4 and 2 <= row < rows + 2:
                total[...] += h0.astype(F32)
                if row < early + 2:
                    h0_ref[row, t - 4] = h0
                else:
                    rest[late + row - early, t - 4] = h0
            act = rms_silu(h0.astype(F32), table[1], mask * keep if t < 4 else mask)
            act_one[row, t] = act.astype(BF16)

        def start(half):
            taps = planes[:, pl.ds(row, 3), half * SLOTS : (half + 1) * SLOTS]
            taps = [taps.reshape(27 * SLOTS, width), jnp.ones((SLOTS, width), F32)]
            taps = jnp.concatenate(taps, axis=0).astype(BF16)
            return jnp.dot(win[...], taps, preferred_element_type=F32)

        return [
            (
                functools.partial(start, half),
                [functools.partial(end, count * half + t, t * channels) for t in range(count)],
            )
            for half in range(2)
        ]

    def middle_units(row):
        def done(dr, t, product):
            mask = row_mask(row + dr, 1, rows + 2)
            h1 = shifted_sum(product, channels) + table[2]
            act = rms_silu(h1, table[3], mask * keep if t < 2 else mask)
            if row + dr < early + 2:
                act_two[row + dr, t] = act.astype(BF16)
            if row + dr >= early:
                rest[row + dr - early, t] = act.astype(BF16)
            kind = min(row + dr, 2) + max(row + dr - rows + 1, 0)
            for later in range(3):
                if 0 <= t - later < count:
                    sums[5 * later + kind] += act

        return pair_units(act_one, mid_parts, row, count + 2, done)

    def loop(begin, end, body):
        for pair in range(begin, end):
            body(pair * 2)

    def inputs(row):
        return first_units(row) + first_units(row + 1)

    last_units, written_units, written, sent = writer(
        act_two, h0_ref, 2, out_parts, table, stage, order, tiles_ref, out_ref, out_hbm, left, 0
    )

    def steady(row, first=True):
        units = mixed(
            written_units(0) + written_units(1) if row else [], middle_units(row + 4)
        )
        units += mixed(last_units(row) if row < early else [], inputs(row + 8) if first else [])
        pipelined(units)
        if row:
            written(row - 2)
            sent(row - 2).start()
        if row + 4 >= early:
            handing(row + 4 - early).start()

    pairs = rows // 2
    pipelined(inputs(0) + inputs(2))
    loop(0, 2, lambda row: pipelined(mixed(middle_units(row), inputs(row + 4))))
    loop(0, pairs - 2, steady)
    for row in range(late + 2, 2 * late + 2, 2):
        handing(row).start()
    steady(rows - 4, first=False)
    if early > rows - 4:
        pipelined(written_units(0) + written_units(1))
        written(early - 2)
        sent(early - 2).start()

    image = total[...] * table[5] + table[4] * table[5] * (count * rows)
    halves = [image[:, :128], image[:, 128:]]
    lane = lax.broadcasted_iota(jnp.int32, (channels, 128), 1)
    for i in range(9):
        down, later = i // 3, i % 3
        read = sums[5 * later + down] + sums[5 * later + down + 1] + sums[5 * later + down + 2]
        left_tap, middle_tap, right_tap = (
            coefs[k, i * channels : (i + 1) * channels] for k in range(3)
        )
        own = left_tap + middle_tap + jnp.where(lane > 0, right_tap, 0.0)
        halves[0] = halves[0] + read[:, :128] * own
        own = middle_tap + right_tap + jnp.where(lane < 127, left_tap, 0.0)
        halves[1] = halves[1] + read[:, 128:] * own
    weighted = jnp.sum(halves[0] + halves[1], keepdims=True)
    sum_ref[...] = jnp.broadcast_to(weighted * flags[4:5, :128], sum_ref.shape)
    for row in range(0, early, 2):
        sent(row).wait()
    for row in range(0, 2 * late + 2, 2):
        handing(row).wait()


def rest_kernel(
    table, out_alone, out_both, out_rest, rest_hbm, begun, out_hbm,
    rest, handed, out_ref, left, stage, order, tiles_ref,
):
    del begun
    late, count, width = out_ref.shape[0], out_ref.shape[1], table.shape[2]
    copies = []
    for i, (row, end, frames) in enumerate(
        ((0, late + 2, count + 2), (late + 2, 2 * late + 2, count))
    ):
        some = pl.ds(row, end - row), pl.ds(0, frames)
        copies.append(pltpu.make_async_copy(rest_hbm.at[some], rest.at[some], handed.at[i]))
    for copy in copies:
        copy.start()
    order_of_pixels(order, stage, width, count)
    last_units, written_units, written, sent = writer(
        rest, rest, late + 2, (out_alone, out_both, out_rest), table, stage, order, tiles_ref,
        out_ref, out_hbm, left, out_hbm.shape[0] - late,
    )
    for copy in copies:
        copy.wait()
    for row in range(0, late + 2, 2):
        units = written_units(0) + written_units(1) if row else []
        pipelined(units + (last_units(row) if row < late else []))
        if row:
            written(row - 2)
            sent(row - 2).start()
    for row in range(0, late, 2):
        sent(row).wait()


def local(
    frames, segments, targets, in_weight, in_bias, gain_one, mid_weight, mid_bias,
    gain_two, out_weight, out_bias, head_weight, head_bias,
):
    count, rows = frames.shape[0], frames.shape[1]
    channels = in_bias.shape[0]
    width = frames.shape[2] // 3
    devices = lax.axis_size(EVERY)

    own = frames.transpose(1, 0, 2)
    previous = moved(own, POSITION, 1)
    oldest = moved(own, POSITION, 2)
    padded = lax.optimization_barrier(jnp.pad(own, ((3, 3), (0, 0), (0, 0))))
    spans = (padded[3 : rows + 3], previous, oldest)
    edge = jnp.concatenate([x[rows - 3 :] for x in spans], axis=0)
    edge, mid_weight, out_weight = lax.optimization_barrier((edge, mid_weight, out_weight))
    low = moved(edge, "band", 1)
    high = moved(jnp.concatenate([x[:3] for x in spans], axis=0), "band", -1)

    win = in_weight.transpose(2, 1, 0, 3).reshape(27, 3, channels).astype(F32)
    win = jnp.pad(win, ((0, 0), (0, SLOTS - 3), (0, 0)))
    clip_row = jnp.pad(segments.astype(F32), (0, channels - segments.shape[0]))
    cols = jnp.stack(
        [in_bias, gain_one, mid_bias, gain_two, out_bias, head_weight, clip_row, in_bias]
    )
    block = 3 * channels
    begin, end = block // 256 * 256, 3 * block // 256 * 256 + 256
    parts = [(block, begin), (2 * block, end - begin), (block, 4 * block - end)] * 2
    vmem = pl.BlockSpec(memory_space=pltpu.VMEM)
    prepared = pl.pallas_call(
        prepared_kernel,
        in_specs=[vmem] * 4,
        out_specs=[vmem] * 10,
        out_shape=[
            jax.ShapeDtypeStruct((8, width), F32),
            jax.ShapeDtypeStruct((count * channels, 28 * SLOTS), BF16),
            jax.ShapeDtypeStruct((6, channels, width), F32),
            jax.ShapeDtypeStruct((3, 3 * block, 128), F32),
        ] + [jax.ShapeDtypeStruct(shape, BF16) for shape in parts],
        compiler_params=pltpu.CompilerParams(vmem_limit_bytes=12 << 20),
        cost_estimate=pl.CostEstimate(flops=10**9, bytes_accessed=6 * 10**6, transcendentals=0),
    )(win, mid_weight.swapaxes(0, 1), out_weight.swapaxes(0, 1), cols)
    late = rows // 6
    early = rows - late
    hbm = pl.BlockSpec(memory_space=pltpu.HBM)
    out = jax.ShapeDtypeStruct((rows, count, width * channels), BF16)

    kept = pltpu.VMEM((2 * late + 2, count + 2, channels, width), BF16)

    def row_buffers(amount):
        return [
            pltpu.VMEM((amount, count, width * channels), BF16),
            pltpu.SemaphoreType.DMA((amount // 2,)),
        ]

    ordering = [
        pltpu.VMEM((2, count, 128, width), BF16),
        pltpu.VMEM((width, width), BF16),
        pltpu.VMEM((2, count, width * channels), F32),
    ]
    features, weighted, rest = pl.pallas_call(
        block_kernel,
        in_specs=[vmem] * 15,
        out_specs=[hbm, vmem, hbm],
        out_shape=[
            out,
            jax.ShapeDtypeStruct((devices, 128), F32),
            jax.ShapeDtypeStruct((HANDED,) + kept.shape[1:], BF16),
        ],
        scratch_shapes=[kept, pltpu.SemaphoreType.DMA((late + 1,))] + row_buffers(early) + [
            pltpu.VMEM((rows + 6, 2 * SLOTS, 3 * width), F32),
            pltpu.VMEM((9, rows + 6, 2 * SLOTS, width), F32),
            pltpu.VMEM((rows + 4, count + 4, channels, width), BF16),
            pltpu.VMEM((early + 2, count + 2, channels, width), BF16),
            pltpu.VMEM((early + 2, count, channels, width), BF16),
            pltpu.VMEM((channels, width), F32),
            pltpu.VMEM((15, channels, width), F32),
        ] + ordering,
        compiler_params=pltpu.CompilerParams(vmem_limit_bytes=32 << 20),
    )(*prepared, padded, previous, oldest, low, high)
    weighted, clip_of = lax.optimization_barrier((weighted, segments))
    gathered = lax.all_to_all(weighted, EVERY, 0, 0, tiled=True)
    table, out_weights = prepared[2], prepared[-3:]
    features = pl.pallas_call(
        rest_kernel,
        in_specs=[vmem] * 4 + [hbm] * 2,
        out_specs=hbm,
        out_shape=out,
        scratch_shapes=[kept, pltpu.SemaphoreType.DMA((2,))] + row_buffers(late) + ordering,
        input_output_aliases={5: 0},
        compiler_params=pltpu.CompilerParams(vmem_limit_bytes=16 << 20),
        cost_estimate=pl.CostEstimate(flops=5 * 10**9, bytes_accessed=10**7, transcendentals=0),
    )(table, *out_weights, rest, features)
    features = features.transpose(1, 0, 2)

    clips = targets.shape[0]
    part = jnp.sum(gathered[:, :clips], axis=0)
    labels = jnp.arange(clips, dtype=jnp.int32)
    member = (clip_of[:, None] == labels[None, :]).astype(F32)
    cells = jnp.sum(member, axis=0) * (count * rows * lax.axis_size("band") * width)
    scores = part / cells + head_bias[0]
    loss = jnp.mean((scores - targets) ** 2)
    return features, scores, loss


def solution(mesh):
    split = P(POSITION, "band", None)
    return jax.shard_map(
        local,
        mesh=mesh,
        in_specs=(split,) + (P(),) * 12,
        out_specs=(split, P(), P()),
        check_vma=False,
    )
```
